128 devices in a mesh: dp: 8 (over z, core), mp: 16 (over y, x).
Axes of the slice: x: 4, y: 4, z: 4, core: 2. Of those that a mesh axis runs over, the one named last changes fastest.
Arguments:
- old_weight: float32 [1536, 43008], P('dp', 'mp'), may hold values from -6 to 6
- old_first: float32 [1536, 43008], P('dp', 'mp'), may hold values from -6 to 6
- old_second: float32 [1536, 43008], P('dp', 'mp'), may hold values from 0.1 to 2
- gradient: float32 [1536, 43008], P('dp', 'mp'), may hold values from -6 to 6
- old_rows: int32 [8, 192], replicated, may hold values from 0 to 1535, as said below
- new_rows: int32 [8, 192], replicated, may hold values from 0 to 1535, as said below
- new_units: int32 [16, 21], replicated, may hold values from 0 to 335, as said below
- step: int32 [1], replicated, may hold values from 1 to 49
Outputs:
- new_weight: float32 [1536, 43008], P('dp', 'mp')
- new_first: float32 [1536, 43008], P('dp', 'mp')
- new_second: float32 [1536, 43008], P('dp', 'mp')
- update: float32 [1536, 43008], P('dp', 'mp')
The draws below stay inside these ranges and needn't reach their ends.
Inputs may be any that keep to these rules, and one draw needn't show every extreme that they name: old_rows names every slab row once. Of the rows in one old data shard, at most 36 are named by any one new data shard, and in every draw each old data shard has exactly 36 for some new data shard. new_rows names every slab row once; the bound on rows from one old data shard to one new data shard, stated for old_rows, holds. new_units names every column unit once. Of the units u * 21 to u * 21 + 20 of old tensor shard u, at most 2 are named by any one new tensor shard, and in every draw each old tensor shard has exactly 2 for some new tensor shard.
All inputs are finite; a program needn't handle non-finite values.
Results may differ from the reference program's by a relative error of at most 0.00018.
Values sent between devices are 32-bit elements; how exact they have to be, the bound alone decides.
No kernel may reach another device: no remote copies, remote signals or barrier semaphores. Data moves between devices by JAX's collectives and lax.ppermute only.
A program may use at most 128 MiB of HBM per device.

```python
import math
import jax
import jax.numpy as jnp

HEAD_DIM = 128
ROWS_DEV = 192
SLAB = 1536
COLS = 43008
UNITS = 336
UNIT_DEV = 21


def shift_weights(key, shards, per_shard):
    base = per_shard // shards
    remain = per_shard % shards
    extra = base // 2
    index_set = jnp.arange(shards, dtype=jnp.int32)
    weights = base + (index_set < remain).astype(jnp.int32)
    weights = weights.at[0].add(extra).at[shards - 1].add(-extra)
    key_move, key_order = jax.random.split(key)
    moved = jax.random.randint(key_move, (), 0, max(extra, 1), dtype=jnp.int32)
    weights = weights.at[1].add(moved).at[shards - 2].add(-moved)
    return weights[jax.random.permutation(key_order, shards)].astype(jnp.int32)


def move_lists(key, shards, per_shard, old_flat):
    keys = jax.random.split(key, 4)
    weights = shift_weights(keys[0], shards, per_shard)
    sigma = jax.random.permutation(keys[1], shards).astype(jnp.int32)
    sigma_inv = jnp.argsort(sigma).astype(jnp.int32)
    source = jnp.arange(shards, dtype=jnp.int32)[:, None]
    target = jnp.arange(shards, dtype=jnp.int32)[None, :]
    counts = weights[(sigma_inv[target] - source) % shards]
    offsets = jnp.cumsum(counts, axis=0) - counts
    orders = jax.vmap(lambda sub: jax.random.permutation(sub, per_shard))(jax.random.split(keys[2], shards)).astype(jnp.int32)
    shuffles = jax.vmap(lambda sub: jax.random.permutation(sub, per_shard))(jax.random.split(keys[3], shards)).astype(jnp.int32)
    cumul = jnp.cumsum(weights).astype(jnp.int32)
    walker = jnp.arange(per_shard, dtype=jnp.int32)
    segment = jnp.searchsorted(cumul, walker, side='right').astype(jnp.int32)
    within = walker - (cumul - weights)[segment]
    dest = sigma[(source + segment[None, :]) % shards]
    arrive = offsets[source, dest] + within[None, :]
    new_slot = shuffles[dest, arrive]
    values = old_flat.reshape(shards, per_shard)[source, orders]
    spots = (dest * per_shard + new_slot).reshape(-1)
    new_flat = jnp.zeros((shards * per_shard,), jnp.int32).at[spots].set(values.reshape(-1).astype(jnp.int32))
    return new_flat.reshape(shards, per_shard)


def row_lists(key):
    shards = SLAB // ROWS_DEV
    old_flat = jax.random.permutation(jax.random.fold_in(key, 11), SLAB).astype(jnp.int32)
    new_list = move_lists(jax.random.fold_in(key, 12), shards, ROWS_DEV, old_flat)
    return (old_flat.reshape(shards, ROWS_DEV), new_list)


def draw_old_rows(key, part):
    both_lists = row_lists(key)
    return both_lists[0]


def draw_new_rows(key, part):
    both_lists = row_lists(key)
    return both_lists[1]


def draw_new_units(key, part):
    key = jax.random.fold_in(key, 3)
    shards = UNITS // UNIT_DEV
    old_flat = jnp.arange(UNITS, dtype=jnp.int32)
    return move_lists(key, shards, UNIT_DEV, old_flat)


def block_scale(stream_key, extent, cuts, least, largest):
    loudness = 1.0
    for axis_at, shards_of in cuts:
        heights = jax.random.uniform(jax.random.fold_in(jax.random.fold_in(stream_key, 6), axis_at), (shards_of,), jnp.float32, least / len(cuts), largest / len(cuts))
        loudness = loudness * jnp.repeat(jnp.exp(heights), extent[axis_at] // shards_of).reshape((-1,) + (1,) * (len(extent) - 1 - axis_at))
    return loudness


def gaussian(key, dims, scale, reach, cuts=(), kind=jnp.bfloat16):
    result = jax.random.normal(key, dims, jnp.float32) * scale
    if len(cuts) > 0:
        result = block_scale(key, dims, cuts, -0.22, 0.18) * result
    return jnp.clip(result, min=-reach, max=reach).astype(kind)


def setup_inputs(seed: int = 0) -> dict:
    key_list = jax.random.split(jax.random.key(seed), 9)
    old_weight = gaussian(key_list[0], (SLAB, COLS), 1.0, 6.0, ((0, 8), (1, 16)), jnp.float32)
    old_first = gaussian(key_list[1], (SLAB, COLS), 1.0, 6.0, ((0, 8), (1, 16)), jnp.float32)
    old_second = jnp.clip(jnp.exp(math.log(2.0) - 2.9957323 * jax.random.uniform(key_list[2], (SLAB, COLS), jnp.float32) ** block_scale(key_list[2], (SLAB, COLS), ((0, 8), (1, 16)), -0.2, 0.2)), 0.1, 2.0)
    gradient = gaussian(key_list[3], (SLAB, COLS), 1.0, 6.0, ((0, 8), (1, 16)), jnp.float32)
    old_rows = draw_old_rows(jax.random.fold_in(key_list[8], 71), 0)
    new_rows = draw_new_rows(jax.random.fold_in(key_list[8], 71), 0)
    new_units = draw_new_units(jax.random.fold_in(key_list[8], 71), 0)
    step = jax.random.randint(key_list[7], (1,), 1, 50).astype(jnp.int32)
    return {"old_weight": old_weight, "old_first": old_first, "old_second": old_second, "gradient": gradient, "old_rows": old_rows, "new_rows": new_rows, "new_units": new_units, "step": step}


beta_one = 0.9
beta_two = 0.999
epsilon = 1e-08
learn_rate = 0.001
decay_rate = 0.1

def adam_step(weight, first, second, gradient, step):
    step_count = step[0].astype(jnp.float32)
    new_first = beta_one * first + (1.0 - beta_one) * gradient
    new_second = beta_two * second + (1.0 - beta_two) * gradient * gradient
    first_fix = 1.0 - jnp.power(jnp.float32(beta_one), step_count)
    second_fix = 1.0 - jnp.power(jnp.float32(beta_two), step_count)
    update = new_first / first_fix / (jnp.sqrt(new_second / second_fix) + epsilon) + decay_rate * weight
    new_weight = weight - learn_rate * update
    return (new_weight, new_first, new_second, update)

def reference(old_weight, old_first, old_second, gradient, old_rows, new_rows, new_units, step):
    old_flat = old_rows.reshape(-1).astype(jnp.int32)
    new_flat = new_rows.reshape(-1).astype(jnp.int32)
    places = jnp.arange(SLAB, dtype=jnp.int32)
    old_place = jnp.zeros((SLAB,), jnp.int32).at[old_flat].set(places)
    picked = old_place[new_flat]
    unit_order = new_units.reshape(-1).astype(jnp.int32)

    def regroup(values):
        values = values[picked]
        values = values.reshape(SLAB, UNITS, HEAD_DIM)[:, unit_order, :]
        return values.reshape(SLAB, UNITS * HEAD_DIM)
    weight = regroup(old_weight)
    first = regroup(old_first)
    second = regroup(old_second)
    return adam_step(weight, first, second, gradient, step)
```

```python
import functools

import jax
import jax.numpy as jnp
from jax import lax
from jax.experimental import pallas as pl
from jax.experimental.pallas import tpu as pltpu
from jax.sharding import PartitionSpec as P

UNIT = 128
ROWS = 192
UNITS = 21
COLS = UNIT * UNITS
DP = 8
MP = 16
ROOM = 40
PAIR = 2
VMEM_LIMIT = 40 * 1024 * 1024

beta_one = 0.9
beta_two = 0.999
epsilon = 1e-08
learn_rate = 0.001
decay_rate = 0.1

MOVES = [(dz, dc) for dz in range(4) for dc in range(2)]
HBM = pl.BlockSpec(memory_space=pl.ANY)
VMEM = pl.BlockSpec(memory_space=pltpu.VMEM)
SMEM = pl.BlockSpec(memory_space=pltpu.SMEM)


def cost(nbytes, flops=0):
    return pl.CostEstimate(flops=flops, bytes_accessed=nbytes, transcendentals=0)


def params():
    return pltpu.CompilerParams(vmem_limit_bytes=VMEM_LIMIT)


def row_plan(old_rows, new_rows):
    d = lax.axis_index("dp")
    z, c = d // 2, d % 2
    shard = jnp.arange(DP, dtype=jnp.int32)
    old_mine = lax.dynamic_index_in_dim(old_rows, d, 0, keepdims=False)
    new_mine = lax.dynamic_index_in_dim(new_rows, d, 0, keepdims=False)
    slots = jnp.arange(DP * ROOM, dtype=jnp.int32)
    earlier = jnp.arange(ROWS)[None, :] < jnp.arange(ROWS)[:, None]

    hit = jnp.any(old_mine[:, None, None] == new_rows[None, :, :], axis=2)
    move_to = ((shard // 2 - z) % 4) * 2 + (shard % 2 + c) % 2
    target = jnp.sum(jnp.where(hit, move_to[None, :], 0), axis=1)
    rank = jnp.sum(((target[:, None] == target[None, :]) & earlier).astype(jnp.int32), axis=1)
    pack = (slots[:, None] == (target * ROOM + rank)[None, :]).astype(jnp.bfloat16)

    equal = new_mine[:, None, None] == old_rows[None, :, :]
    mine = jnp.any(equal, axis=0)
    before = jnp.sum((mine[:, None, :] & earlier[None, :, :]).astype(jnp.int32), axis=2)
    move_from = ((z - shard // 2) % 4) * 2 + (shard % 2 + c) % 2
    value = move_from[:, None] * ROOM + before
    source = jnp.sum(jnp.where(equal, value[None], 0), axis=(1, 2))
    unpack = (source[:, None] == slots[None, :]).astype(jnp.bfloat16)
    return pack, unpack


def unit_plan(new_units):
    m = lax.axis_index("mp")
    own = jnp.arange(UNITS, dtype=jnp.int32)
    slots = jnp.arange(MP * PAIR, dtype=jnp.int32)

    hit = jnp.any((m * UNITS + own)[:, None, None] == new_units[None, :, :], axis=2)
    target = jnp.sum(jnp.where(hit, jnp.arange(MP, dtype=jnp.int32)[None, :], 0), axis=1)
    earlier = own[None, :] < own[:, None]
    rank = jnp.sum(((target[:, None] == target[None, :]) & earlier).astype(jnp.int32), axis=1)
    here = (target * PAIR + rank)[None, :] == slots[:, None]
    send = jnp.sum(jnp.where(here, own[None, :], 0), axis=1)

    wanted = lax.dynamic_index_in_dim(new_units, m, 0, keepdims=False)
    origin = wanted // UNITS
    lower = (origin[:, None] == origin[None, :]) & (wanted[None, :] < wanted[:, None])
    take = origin * PAIR + jnp.sum(lower.astype(jnp.int32), axis=1)
    return send, take


def select_rows(onehot, values):
    high = values.astype(jnp.bfloat16)
    rest = values - high.astype(jnp.float32)
    middle = rest.astype(jnp.bfloat16)
    low = (rest - middle.astype(jnp.float32)).astype(jnp.bfloat16)
    dot = functools.partial(jnp.dot, preferred_element_type=jnp.float32)
    return (dot(onehot, high) + dot(onehot, middle)) + dot(onehot, low)


def unit_pack_kernel(send, x, out, sems):
    copies = []
    for s in range(MP * PAIR):
        columns = pl.ds(pl.multiple_of(send[s] * UNIT, UNIT), UNIT)
        copies.append(pltpu.make_async_copy(x.at[:, columns], out.at[s], sems.at[s]))
    for copy in copies:
        copy.start()
    for copy in copies:
        copy.wait()


def unit_pack(x, send):
    out = pl.pallas_call(
        unit_pack_kernel,
        out_shape=jax.ShapeDtypeStruct((MP * PAIR, ROWS, UNIT), jnp.float32),
        in_specs=[SMEM, HBM],
        out_specs=HBM,
        scratch_shapes=[pltpu.SemaphoreType.DMA((MP * PAIR,))],
        compiler_params=params(),
        cost_estimate=cost(6 * 2**20),
        name="unit_pack",
    )(send, x)
    return out.reshape(MP, PAIR, ROWS, UNIT)


WIDE = 3 * UNIT


def row_pack_kernel(onehot, x, *outs):
    picked = select_rows(onehot[...], x[...])
    for i, out in enumerate(outs):
        out[...] = picked[i * ROOM : (i + 1) * ROOM]


MESSAGES = [jax.ShapeDtypeStruct((ROOM, COLS), jnp.float32)] * DP


def row_pack(x, onehot):
    return pl.pallas_call(
        row_pack_kernel,
        out_shape=MESSAGES,
        grid=(COLS // WIDE,),
        in_specs=[
            pl.BlockSpec((DP * ROOM, ROWS), lambda i: (0, 0)),
            pl.BlockSpec((ROWS, WIDE), lambda i: (0, i)),
        ],
        out_specs=[pl.BlockSpec((ROOM, WIDE), lambda i: (0, i))] * DP,
        compiler_params=params(),
        cost_estimate=cost(6 * 2**20, 3 * 2 * 320 * 192 * COLS),
        name="row_pack",
    )(onehot, x)


def unit_row_pack_kernel(take, onehot, recv, *rest):
    outs, wide, sems = rest[:DP], rest[DP], rest[DP + 1]
    i = pl.program_id(0)
    width = WIDE // UNIT

    def copy_of(j):
        columns = pl.ds(j * UNIT, UNIT)
        return pltpu.make_async_copy(recv.at[take[j]], wide.at[:, columns], sems.at[j])

    @pl.when(i == 0)
    def _():
        for j in range(UNITS):
            copy_of(j).start()

    for step in range(COLS // WIDE):

        @pl.when(i == step)
        def _(step=step):
            for j in range(step * width, (step + 1) * width):
                copy_of(j).wait()
            picked = select_rows(onehot[...], wide[:, step * WIDE : (step + 1) * WIDE])
            for k, out in enumerate(outs):
                out[...] = picked[k * ROOM : (k + 1) * ROOM]


def unit_row_pack(recv, take, onehot):
    return pl.pallas_call(
        unit_row_pack_kernel,
        out_shape=MESSAGES,
        grid=(COLS // WIDE,),
        in_specs=[SMEM, pl.BlockSpec((DP * ROOM, ROWS), lambda i: (0, 0)), HBM],
        out_specs=[pl.BlockSpec((ROOM, WIDE), lambda i: (0, i))] * DP,
        scratch_shapes=[
            pltpu.VMEM((ROWS, COLS), jnp.float32),
            pltpu.SemaphoreType.DMA((UNITS,)),
        ],
        compiler_params=params(),
        cost_estimate=cost(6 * 2**20, 3 * 2 * 320 * 192 * COLS),
        name="unit_row_pack",
    )(take, onehot, recv.reshape(MP * PAIR, ROWS, UNIT))


def joined(parts):
    return jnp.concatenate([p[...] for p in parts], axis=0)


def row_unit_pack_kernel(send, onehot, *rest):
    parts, out, held, sems = rest[:DP], rest[DP], rest[DP + 1], rest[DP + 2]
    i = pl.program_id(0)
    picked = select_rows(onehot[...], joined(parts))
    width = WIDE // UNIT
    for k in range(width):
        held[i * width + k] = picked[:, k * UNIT : (k + 1) * UNIT]

    @pl.when(i == COLS // WIDE - 1)
    def _():
        copies = []
        for s in range(MP * PAIR):
            copies.append(pltpu.make_async_copy(held.at[send[s]], out.at[s], sems.at[s]))
        for copy in copies:
            copy.start()
        for copy in copies:
            copy.wait()


def row_unit_pack(parts, send, onehot):
    out = pl.pallas_call(
        row_unit_pack_kernel,
        out_shape=jax.ShapeDtypeStruct((MP * PAIR, ROWS, UNIT), jnp.float32),
        grid=(COLS // WIDE,),
        in_specs=[SMEM, pl.BlockSpec((ROWS, DP * ROOM), lambda i: (0, 0))]
        + [pl.BlockSpec((ROOM, WIDE), lambda i: (0, i))] * DP,
        out_specs=HBM,
        scratch_shapes=[
            pltpu.VMEM((UNITS, ROWS, UNIT), jnp.float32),
            pltpu.SemaphoreType.DMA((MP * PAIR,)),
        ],
        compiler_params=params(),
        cost_estimate=cost(7 * 2**20, 3 * 2 * 320 * 192 * COLS),
        name="row_unit_pack",
    )(send, onehot, *parts)
    return out.reshape(MP, PAIR, ROWS, UNIT)


def moment_kernel(is_first, onehot, gradient, *rest):
    parts, out = rest[:DP], rest[DP]
    picked = select_rows(onehot[...], joined(parts))
    g = gradient[...]
    if is_first:
        out[...] = beta_one * picked + (1.0 - beta_one) * g
    else:
        out[...] = beta_two * picked + (1.0 - beta_two) * g * g


def moment(parts, onehot, gradient, is_first):
    block = pl.BlockSpec((ROWS, WIDE), lambda i: (0, i))
    return pl.pallas_call(
        functools.partial(moment_kernel, is_first),
        out_shape=jax.ShapeDtypeStruct((ROWS, COLS), jnp.float32),
        grid=(COLS // WIDE,),
        in_specs=[pl.BlockSpec((ROWS, DP * ROOM), lambda i: (0, 0)), block]
        + [pl.BlockSpec((ROOM, WIDE), lambda i: (0, i))] * DP,
        out_specs=block,
        compiler_params=params(),
        cost_estimate=cost(7 * 2**20, 3 * 2 * 320 * 192 * COLS),
        name="new_first" if is_first else "new_second",
    )(onehot, gradient, *parts)


def update_kernel(take, fixes, recv, first, second, new_weight, update, wide, sems):
    i = pl.program_id(0)
    width = WIDE // UNIT

    def copy_of(j):
        columns = pl.ds(j * UNIT, UNIT)
        return pltpu.make_async_copy(recv.at[take[j]], wide.at[:, columns], sems.at[j])

    @pl.when(i == 0)
    def _():
        for j in range(UNITS):
            copy_of(j).start()

    for step in range(COLS // WIDE):

        @pl.when(i == step)
        def _(step=step):
            for j in range(step * width, (step + 1) * width):
                copy_of(j).wait()
            weight = wide[:, step * WIDE : (step + 1) * WIDE]
            root = jnp.sqrt(second[...] / fixes[1]) + epsilon
            change = first[...] / fixes[0] / root + decay_rate * weight
            update[...] = change
            new_weight[...] = weight - learn_rate * change


def weight_update(recv, take, fixes, first, second):
    block = pl.BlockSpec((ROWS, WIDE), lambda i: (0, i))
    return pl.pallas_call(
        update_kernel,
        out_shape=[jax.ShapeDtypeStruct((ROWS, COLS), jnp.float32)] * 2,
        grid=(COLS // WIDE,),
        in_specs=[SMEM, SMEM, HBM, block, block],
        out_specs=[block, block],
        scratch_shapes=[
            pltpu.VMEM((ROWS, COLS), jnp.float32),
            pltpu.SemaphoreType.DMA((UNITS,)),
        ],
        compiler_params=params(),
        cost_estimate=cost(10 * 2**20),
        name="weight_update",
    )(take, fixes, recv.reshape(MP * PAIR, ROWS, UNIT), first, second)


def swap_rows(messages):
    arrived = []
    for message, (dz, dc) in zip(messages, MOVES):
        if dz == 0 and dc == 0:
            arrived.append(message)
            continue
        pairs = [(z * 2 + c, (z + dz) % 4 * 2 + (c + dc) % 2) for z in range(4) for c in range(2)]
        arrived.append(lax.ppermute(message, "dp", pairs))
    return arrived


def swap_units(packed):
    return lax.all_to_all(packed, "mp", split_axis=0, concat_axis=0, tiled=True)


def body(old_weight, old_first, old_second, gradient, old_rows, new_rows, new_units, step):
    send, take = unit_plan(new_units)
    pack, unpack = row_plan(old_rows, new_rows)
    count = step[0].astype(jnp.float32)
    fixes = jnp.stack(
        [
            1.0 - jnp.power(jnp.float32(beta_one), count),
            1.0 - jnp.power(jnp.float32(beta_two), count),
        ]
    )

    first_units = swap_units(unit_pack(old_first, send))
    weight_rows = swap_rows(row_pack(old_weight, pack))
    second_units = swap_units(unit_pack(old_second, send))
    first_rows = swap_rows(unit_row_pack(first_units, take, pack))
    weight_units = swap_units(row_unit_pack(weight_rows, send, unpack))
    second_rows = swap_rows(unit_row_pack(second_units, take, pack))

    new_first = moment(first_rows, unpack, gradient, True)
    new_second = moment(second_rows, unpack, gradient, False)
    new_weight, update = weight_update(weight_units, take, fixes, new_first, new_second)
    return new_weight, new_first, new_second, update


def solution(mesh):
    return jax.shard_map(
        body,
        mesh=mesh,
        in_specs=(P("dp", "mp"), P("dp", "mp"), P("dp", "mp"), P("dp", "mp"), P(), P(), P(), P()),
        out_specs=(P("dp", "mp"), P("dp", "mp"), P("dp", "mp"), P("dp", "mp")),
        check_vma=False,
    )
```

```python
import functools

import jax
import jax.numpy as jnp
from jax import lax
from jax.experimental import pallas as pl
from jax.experimental.pallas import tpu as pltpu
from jax.sharding import PartitionSpec as P

UNIT = 128
HALF = UNIT // 2
ROWS = 192
FOLD = ROWS // 2
UNITS = 21
COLS = UNIT * UNITS
DP = 8
MP = 16
ROOM = 36
PAIR = 2
SLOTS = MP * PAIR
BLOCK = ROWS + FOLD
TILES = 32
WIDE = TILES // 2 * UNIT
MESSAGE = 2 * ROOM
STACK = DP * MESSAGE
PAIRS = TILES - UNITS
CHUNK = 4
VMEM_LIMIT = 24 * 1024 * 1024

beta_one = 0.9
beta_two = 0.999
epsilon = 1e-08
learn_rate = 0.001
decay_rate = 0.1

MOVES = [(0, 0), (0, 1), (1, 0), (3, 0), (1, 1), (3, 1), (2, 0), (2, 1)]
HBM = pl.BlockSpec(memory_space=pltpu.HBM)
ANY = pl.BlockSpec(memory_space=pl.ANY)
VMEM = pl.BlockSpec(memory_space=pltpu.VMEM)
SMEM = pl.BlockSpec(memory_space=pltpu.SMEM)


def f32(*shape):
    return jax.ShapeDtypeStruct(shape, jnp.float32)


def call(kernel, name, ins, outs, out_shape, scratch, mebibytes, *args):
    return pl.pallas_call(
        kernel,
        out_shape=out_shape,
        in_specs=ins,
        out_specs=outs,
        scratch_shapes=scratch,
        compiler_params=pltpu.CompilerParams(vmem_limit_bytes=VMEM_LIMIT),
        cost_estimate=pl.CostEstimate(
            flops=0, bytes_accessed=mebibytes * 2**20, transcendentals=0
        ),
        name=name,
    )(*args)


def row_plan_kernel(place, old, new, new_turned, pack, take):
    d = place[0]
    z, c = d // 2, d % 2
    old_mine = old[pl.ds(d, 1), :]
    lane = lax.broadcasted_iota(jnp.int32, (ROWS, DP), 1)
    new_mine = jnp.sum(jnp.where(lane == d, new_turned[...], 0), axis=1, keepdims=True)
    here = lax.broadcasted_iota(jnp.int32, (ROWS, ROWS), 0)
    there = lax.broadcasted_iota(jnp.int32, (ROWS, ROWS), 1)
    earlier = (here < there).astype(jnp.float32).astype(jnp.bfloat16)

    goes, comes = [], []
    for s in range(DP):
        hit = (new_turned[:, s : s + 1] == old_mine).astype(jnp.float32)
        goes.append(jnp.max(hit, axis=0, keepdims=True))
        hit = (new_mine == old[s : s + 1, :]).astype(jnp.float32)
        comes.append(jnp.max(hit, axis=0, keepdims=True))
    both = jnp.concatenate(goes + comes, axis=0)
    before = jnp.dot(both.astype(jnp.bfloat16), earlier, preferred_element_type=jnp.float32)
    both = both.astype(jnp.int32)
    before = before.astype(jnp.int32)

    def first_slot(dz, dc):
        at = 0
        for k, move in enumerate(MOVES):
            at = jnp.where((dz == move[0]) & (dc == move[1]), k * MESSAGE, at)
        return at

    slot = jnp.zeros((1, ROWS), jnp.int32)
    origin = jnp.zeros((ROWS, ROWS), jnp.int32)
    for s in range(DP):
        core = (s % 2 + c) % 2
        to = first_slot((s // 2 - z + 4) % 4, core)
        slot = slot + both[s : s + 1] * (to + before[s : s + 1])
        source = first_slot((z - s // 2 + 4) % 4, core)
        value = source + before[DP + s : DP + s + 1]
        origin = origin + jnp.where(new_mine == old[s : s + 1, :], value, 0)
    origin = jnp.sum(origin, axis=1, keepdims=True)

    def onehot(equal):
        return equal.astype(jnp.float32).astype(jnp.bfloat16)

    index = lax.broadcasted_iota(jnp.int32, (STACK, ROWS), 0)
    pack[0] = onehot(index == slot)
    pack[1] = onehot(index == slot + ROOM)
    index = lax.broadcasted_iota(jnp.int32, (ROWS, STACK), 1)
    take[:ROWS] = onehot(index == origin)
    take[ROWS:] = onehot(index == origin + ROOM)


def row_plan(old_rows, new_rows):
    place = lax.axis_index("dp").astype(jnp.int32).reshape(1)
    pack = jax.ShapeDtypeStruct((2, STACK, ROWS), jnp.bfloat16)
    take = jax.ShapeDtypeStruct((2 * ROWS, STACK), jnp.bfloat16)
    return call(
        row_plan_kernel,
        "row_plan",
        [SMEM, VMEM, VMEM, VMEM],
        [VMEM] * 2,
        [pack, take],
        [],
        1,
        place,
        old_rows,
        new_rows,
        new_rows.T,
    )


def unit_plan_kernel(place, units, turned, send, take):
    m = place[0]
    lane = lax.broadcasted_iota(jnp.int32, (1, UNIT), 1)
    line = lax.broadcasted_iota(jnp.int32, (UNITS, 1), 0)
    earlier = line < lane

    to_row = jnp.zeros((UNITS, UNIT), jnp.int32)
    to_column = jnp.zeros((UNITS, UNITS), jnp.int32)
    for t in range(1, MP):
        to_row = to_row + jnp.where(turned[:, t : t + 1] == m * UNITS + lane, t, 0)
        to_column = to_column + jnp.where(units[t : t + 1, :] == m * UNITS + line, t, 0)
    to_row = jnp.sum(to_row, axis=0, keepdims=True)
    to_column = jnp.sum(to_column, axis=1, keepdims=True)
    rank = jnp.sum(((to_row == to_column) & earlier).astype(jnp.int32), axis=0, keepdims=True)
    send[...] = to_row * PAIR + rank

    row = units[pl.ds(m, 1), :]
    column = lax.broadcasted_iota(jnp.int32, (UNITS, MP), 1) == m
    column = jnp.sum(jnp.where(column, turned[...], 0), axis=1, keepdims=True)
    from_row, from_column = jnp.zeros_like(row), jnp.zeros_like(column)
    for t in range(1, MP):
        from_row = from_row + (row >= t * UNITS).astype(jnp.int32)
        from_column = from_column + (column >= t * UNITS).astype(jnp.int32)
    lower = (from_row == from_column) & (column < row)
    take[...] = from_row * PAIR + jnp.sum(lower.astype(jnp.int32), axis=0, keepdims=True)


def unit_plan(new_units):
    place = lax.axis_index("mp").astype(jnp.int32).reshape(1)
    return call(
        unit_plan_kernel,
        "unit_plan",
        [SMEM, VMEM, VMEM],
        [VMEM] * 2,
        [jax.ShapeDtypeStruct((1, n), jnp.int32) for n in (UNIT, UNITS)],
        [],
        1,
        place,
        new_units,
        new_units.T,
    )


def terms(values):
    high = values.astype(jnp.bfloat16)
    rest = values - high.astype(jnp.float32)
    middle = rest.astype(jnp.bfloat16)
    low = (rest - middle.astype(jnp.float32)).astype(jnp.bfloat16)
    return high, middle, low


def select_rows(onehot, split):
    dot = functools.partial(jnp.dot, preferred_element_type=jnp.float32)
    return (dot(onehot, split[0]) + dot(onehot, split[1])) + dot(onehot, split[2])


def columns_of(u):
    return slice(u * UNIT, (u + 1) * UNIT)


def swapped(x):
    return pltpu.roll(x, HALF, 1)


def left_lanes(rows):
    return lax.broadcasted_iota(jnp.int32, (rows, UNIT), 1) < HALF


def folded(x, upper):
    first, last = x[:FOLD], x[FOLD:]
    if upper:
        return jnp.where(left_lanes(FOLD), swapped(first), last)
    return jnp.where(left_lanes(FOLD), first, swapped(last))


def unfolded(y, upper):
    if upper:
        return jnp.concatenate([swapped(y), y], axis=0)
    return jnp.concatenate([y, swapped(y)], axis=0)


def pack_rows(tile, pack, outs):
    for i in range(0, TILES // 2, CHUNK):
        left = jnp.concatenate([tile(n) for n in range(i, i + CHUNK)], axis=1)
        right = jnp.concatenate([tile(TILES // 2 + n) for n in range(i, i + CHUNK)], axis=1)
        packed = select_rows(pack[0], terms(left)) + select_rows(pack[1], terms(right))
        for k, out in enumerate(outs):
            out[:, i * UNIT : (i + CHUNK) * UNIT] = packed[k * MESSAGE : (k + 1) * MESSAGE]


def take_rows(parts, take, put):
    for i in range(0, TILES // 2, CHUNK):
        columns = slice(i * UNIT, (i + CHUNK) * UNIT)
        values = jnp.concatenate([p[:, columns] for p in parts], axis=0)
        picked = select_rows(take[...], terms(values))
        for k in range(CHUNK):
            put(i + k, picked[:ROWS, columns_of(k)])
            put(TILES // 2 + i + k, picked[ROWS:, columns_of(k)])


class Copies:
    def __init__(self, sems):
        self.sems, self.waiting = sems, []

    def start(self, source, target):
        copy = pltpu.make_async_copy(source, target, self.sems.at[len(self.waiting)])
        copy.start()
        self.waiting.append(copy)
        return copy

    def wait(self):
        for copy in self.waiting:
            copy.wait()


PARTS = 3


class Loads:
    def __init__(self, sems):
        self.sems, self.arrays = sems, []

    def start(self, source, target):
        parts = []
        for i in range(PARTS):
            columns = slice(i * COLS // PARTS, (i + 1) * COLS // PARTS)
            sem = self.sems.at[len(self.arrays) * PARTS + i]
            parts.append(
                pltpu.make_async_copy(source.at[:, columns], target.at[:, columns], sem)
            )
            parts[-1].start()
        self.arrays.append(parts)

    def wait(self, array, unit):
        parts = self.arrays[array]
        for i in range(unit * PARTS // UNITS + 1):
            if parts[i] is not None:
                parts[i].wait()
                parts[i] = None


MESSAGES = [f32(MESSAGE, WIDE)] * DP
SLOT_ARRAY = pltpu.HBM((SLOTS, BLOCK, UNIT), jnp.float32)
SLOT_SPEC = HBM
ARRAY = pltpu.VMEM((ROWS, COLS), jnp.float32)
FOLDS = pltpu.VMEM((UNITS, FOLD, UNIT), jnp.float32)
HELD = pltpu.VMEM((UNITS, ROWS, UNIT), jnp.float32)


def dma(n):
    return pltpu.SemaphoreType.DMA((n,))


def unit_pack_kernel(send, whole, half, out, whole_here, half_here, folds, loads, stores):
    loads, stores = Loads(loads), Copies(stores)
    loads.start(whole, whole_here)
    loads.start(half, half_here)
    for u in range(UNITS):
        loads.wait(0, u)
        stores.start(whole_here.at[:, columns_of(u)], out.at[send[0, u], pl.ds(0, ROWS)])
    for u in range(UNITS):
        loads.wait(1, u)
        folds[u] = folded(half_here[:, columns_of(u)], True)
        stores.start(folds.at[u], out.at[send[0, u], pl.ds(ROWS, FOLD)])
    stores.wait()


def unit_pack(whole, half, send):
    return call(
        unit_pack_kernel,
        "unit_pack",
        [SMEM, HBM, HBM],
        SLOT_SPEC,
        SLOT_ARRAY,
        [ARRAY, ARRAY, FOLDS, dma(2 * PARTS), dma(2 * UNITS)],
        9,
        send,
        whole,
        half,
    )


def row_pack_kernel(pack, whole, half, *rest):
    outs, (whole_here, half_here, loads) = rest[:DP], rest[DP:]
    loads = Loads(loads)
    loads.start(whole, whole_here)
    loads.start(half, half_here)

    def unit(k, u):
        u = min(u, UNITS - 1)
        loads.wait(k, u)
        return (whole_here, half_here)[k][:, columns_of(u)]

    def tile(n):
        if n < UNITS:
            return unit(0, n)
        u = 2 * (n - UNITS)
        return jnp.where(left_lanes(ROWS), unit(1, u), swapped(unit(1, u + 1)))

    pack_rows(tile, pack, outs)


def row_pack(whole, half, pack):
    return call(
        row_pack_kernel,
        "row_pack",
        [VMEM, HBM, HBM],
        [VMEM] * DP,
        MESSAGES,
        [ARRAY, ARRAY, dma(2 * PARTS)],
        9,
        pack,
        whole,
        half,
    )


def unit_row_pack_kernel(take, pack, recv, *rest):
    outs, (here, sems) = rest[:DP], rest[DP:]
    copies, arriving = Copies(sems), {}
    for i in range(0, TILES // 2, CHUNK):
        for n in [*range(i, i + CHUNK), *range(TILES // 2 + i, TILES // 2 + i + CHUNK)]:
            if n < UNITS:
                arriving[n] = copies.start(recv.at[take[0, n]], here.at[n])

    def unit(u):
        if u in arriving:
            arriving.pop(u).wait()
        return here.at[u]

    def tile(n):
        if n < UNITS:
            return unit(n)[:ROWS]
        u = 2 * (n - UNITS)
        a = unfolded(unit(u)[ROWS:], False)
        b = unfolded(unit(min(u + 1, UNITS - 1))[ROWS:], True)
        return jnp.where(left_lanes(ROWS), a, b)

    pack_rows(tile, pack, outs)


def unit_row_pack(recv, take, pack):
    return call(
        unit_row_pack_kernel,
        "unit_row_pack",
        [SMEM, VMEM, ANY],
        [VMEM] * DP,
        MESSAGES,
        [pltpu.VMEM((UNITS, BLOCK, UNIT), jnp.float32), dma(UNITS)],
        10,
        take,
        pack,
        recv,
    )


def row_unit_pack_kernel(send, take, *rest):
    parts, (out, held, folds, sems) = rest[:DP], rest[DP:]
    copies = Copies(sems)

    def put(n, tile):
        if n < UNITS:
            held[n] = tile
            copies.start(held.at[n], out.at[send[0, n], pl.ds(0, ROWS)])
            return
        for u, upper in ((2 * (n - UNITS), False), (2 * (n - UNITS) + 1, True)):
            if u < UNITS:
                folds[u] = folded(tile, upper)
                copies.start(folds.at[u], out.at[send[0, u], pl.ds(ROWS, FOLD)])

    take_rows(parts, take, put)
    copies.wait()


def row_unit_pack(parts, send, take):
    return call(
        row_unit_pack_kernel,
        "row_unit_pack",
        [SMEM] + [VMEM] * (1 + DP),
        SLOT_SPEC,
        SLOT_ARRAY,
        [HELD, FOLDS, dma(2 * UNITS)],
        10,
        send,
        take,
        *parts,
    )


def first_kernel(gradient, take, *rest):
    parts, (first, half, held, half_held, sems) = rest[:DP], rest[DP:]
    copies = Copies(sems)

    def put(n, tile):
        if n < UNITS:
            columns = columns_of(n)
            moment = beta_one * tile + (1.0 - beta_one) * gradient[:, columns]
            held[:, columns] = moment
            copies.start(held.at[:, columns], first.at[:, columns])
        else:
            half_held[n - UNITS] = tile
            copies.start(half_held.at[n - UNITS], half.at[n - UNITS])

    take_rows(parts, take, put)
    copies.wait()


def first_moment(parts, take, gradient):
    return call(
        first_kernel,
        "first_moment",
        [VMEM] * (2 + DP),
        [HBM, HBM],
        [pltpu.HBM((ROWS, COLS), jnp.float32), pltpu.HBM((PAIRS, ROWS, UNIT), jnp.float32)],
        [ARRAY, pltpu.VMEM((PAIRS, ROWS, UNIT), jnp.float32), dma(TILES)],
        11,
        gradient,
        take,
        *parts,
    )


def update_kernel(take, fixes, recv, first, half, gradient, *rest):
    outs, helds, rest = rest[:3], rest[3:6], rest[6:]
    here, first_here, half_here, gradient_here, whole_loads, unit_loads, stores = rest
    loads, whole, stores = Copies(unit_loads), Loads(whole_loads), Copies(stores)
    arrivals = [loads.start(recv.at[take[0, u]], here.at[u]) for u in range(UNITS // 3)]
    whole.start(gradient, gradient_here)
    whole.start(first, first_here)
    halves = loads.start(half, half_here)
    arrivals += [loads.start(recv.at[take[0, u]], here.at[u]) for u in range(UNITS // 3, UNITS)]
    for u in range(UNITS):
        arrivals[u].wait()
        columns = columns_of(u)
        weight = here[u, :ROWS]
        lower = unfolded(here[u, ROWS:], False)
        if u == 0:
            halves.wait()
        upper = half_here[u // 2]
        if u % 2 == 0:
            upper = swapped(upper)
        second = jnp.where(left_lanes(ROWS), lower, upper)
        whole.wait(0, u)
        g = gradient_here[:, columns]
        second = beta_two * second + (1.0 - beta_two) * g * g
        root = jnp.sqrt(second / fixes[1]) + epsilon
        whole.wait(1, u)
        update = first_here[:, columns] / fixes[0] / root + decay_rate * weight
        for held, out, value in zip(helds, outs, (weight - learn_rate * update, second, update)):
            held[:, columns] = value
            stores.start(held.at[:, columns], out.at[:, columns])
    stores.wait()


def weight_update(recv, take, fixes, first, half, gradient):
    return call(
        update_kernel,
        "weight_update",
        [SMEM, SMEM, ANY] + [HBM] * 3,
        [HBM] * 3,
        [f32(ROWS, COLS)] * 3,
        [ARRAY] * 3
        + [
            pltpu.VMEM((UNITS, BLOCK, UNIT), jnp.float32),
            ARRAY,
            pltpu.VMEM((PAIRS, ROWS, UNIT), jnp.float32),
            ARRAY,
            dma(2 * PARTS),
            dma(UNITS + 1),
            dma(3 * UNITS),
        ],
        16,
        take,
        fixes,
        recv,
        first,
        half,
        gradient,
    )


def swap_rows(parts):
    arrived = []
    for part, (dz, dc) in zip(parts, MOVES):
        pairs = [(z * 2 + c, (z + dz) % 4 * 2 + (c + dc) % 2) for z in range(4) for c in range(2)]
        arrived.append(lax.ppermute(part, "dp", pairs) if dz or dc else part)
    return arrived


def swap_units(packed):
    packed = packed.reshape(MP, PAIR, BLOCK, UNIT)
    arrived = lax.all_to_all(packed, "mp", split_axis=0, concat_axis=0, tiled=True)
    return arrived.reshape(SLOTS, BLOCK, UNIT)


def body(old_weight, old_first, old_second, gradient, old_rows, new_rows, new_units, step):
    send, take_units = unit_plan(new_units)
    pack, take = row_plan(old_rows, new_rows)
    in_hbm = functools.partial(pltpu.with_memory_space_constraint, memory_space=pltpu.HBM)
    count = step[0].astype(jnp.float32)
    fixes = jnp.stack(
        [
            1.0 - jnp.power(jnp.float32(beta_one), count),
            1.0 - jnp.power(jnp.float32(beta_two), count),
        ]
    )

    units = swap_units(unit_pack(in_hbm(old_first), in_hbm(old_second), send))
    rows = swap_rows(row_pack(in_hbm(old_weight), in_hbm(old_second), pack))
    packed = row_unit_pack(rows, send, take)
    units, packed = lax.optimization_barrier((units, packed))

    units_two = swap_units(packed)
    rows_two = swap_rows(unit_row_pack(units, take_units, pack))

    new_first, half = first_moment(rows_two, take, gradient)
    new_weight, new_second, update = weight_update(
        units_two, take_units, fixes, in_hbm(new_first), in_hbm(half), in_hbm(gradient)
    )
    return new_weight, new_first, new_second, update


def solution(mesh):
    return jax.shard_map(
        body,
        mesh=mesh,
        in_specs=(P("dp", "mp"), P("dp", "mp"), P("dp", "mp"), P("dp", "mp"), P(), P(), P(), P()),
        out_specs=(P("dp", "mp"), P("dp", "mp"), P("dp", "mp"), P("dp", "mp")),
        check_vma=False,
    )
```

```python
import functools

import jax
import jax.numpy as jnp
from jax import lax
from jax.experimental import pallas as pl
from jax.experimental.pallas import tpu as pltpu
from jax.sharding import PartitionSpec as P

UNIT = 128
HALF = UNIT // 2
ROWS = 192
FOLD = ROWS // 2
UNITS = 21
COLS = UNIT * UNITS
DP = 8
MP = 16
ROOM = 36
PAIR = 2
SLOTS = MP * PAIR
BLOCK = ROWS + FOLD
TILES = 32
WIDE = TILES // 2 * UNIT
MAIN = 32
REST = ROOM - MAIN
MESSAGE = 2 * ROOM
PAIRS = TILES - UNITS
CHUNK = 4
VMEM_LIMIT = 24 * 1024 * 1024

beta_one = 0.9
beta_two = 0.999
epsilon = 1e-08
learn_rate = 0.001
decay_rate = 0.1

MOVES = [(0, 0), (0, 1), (2, 0), (2, 1), (1, 0), (3, 0), (1, 1), (3, 1)]
HBM = pl.BlockSpec(memory_space=pltpu.HBM)
ANY = pl.BlockSpec(memory_space=pl.ANY)
VMEM = pl.BlockSpec(memory_space=pltpu.VMEM)
SMEM = pl.BlockSpec(memory_space=pltpu.SMEM)


def f32(*shape):
    return jax.ShapeDtypeStruct(shape, jnp.float32)


def call(kernel, name, ins, outs, out_shape, scratch, mebibytes, *args):
    return pl.pallas_call(
        kernel,
        out_shape=out_shape,
        in_specs=ins,
        out_specs=outs,
        scratch_shapes=scratch,
        compiler_params=pltpu.CompilerParams(vmem_limit_bytes=VMEM_LIMIT),
        cost_estimate=pl.CostEstimate(
            flops=0, bytes_accessed=mebibytes * 2**20, transcendentals=0
        ),
        name=name,
    )(*args)


def turned(row):
    n = row.shape[1]
    here = lax.broadcasted_iota(jnp.int32, (n, n), 0)
    there = lax.broadcasted_iota(jnp.int32, (n, n), 1)
    return jnp.sum(jnp.where(here == there, row, 0), axis=1, keepdims=True)


def row_plan_kernel(place, old, new, pack, pack_rest, take, take_rest):
    d = place[0]
    z, c = d // 2, d % 2
    old_mine = old[pl.ds(d, 1), :]
    new_mine = turned(new[pl.ds(d, 1), :])
    here = lax.broadcasted_iota(jnp.int32, (ROWS, ROWS), 0)
    there = lax.broadcasted_iota(jnp.int32, (ROWS, ROWS), 1)
    earlier = (here < there).astype(jnp.float32).astype(jnp.bfloat16)

    goes, comes = [], []
    for s in range(DP):
        hit = (turned(new[s : s + 1, :]) == old_mine).astype(jnp.float32)
        goes.append(jnp.max(hit, axis=0, keepdims=True))
        hit = (new_mine == old[s : s + 1, :]).astype(jnp.float32)
        comes.append(jnp.max(hit, axis=0, keepdims=True))
    both = jnp.concatenate(goes + comes, axis=0)
    before = jnp.dot(both.astype(jnp.bfloat16), earlier, preferred_element_type=jnp.float32)
    both = both.astype(jnp.int32)
    before = before.astype(jnp.int32)

    def message(dz, dc):
        at = 0
        for k, move in enumerate(MOVES):
            at = jnp.where((dz == move[0]) & (dc == move[1]), k, at)
        return at

    goes = jnp.zeros((1, ROWS), jnp.int32)
    comes = jnp.zeros((ROWS, ROWS), jnp.int32)
    for s in range(DP):
        core = (s % 2 + c) % 2
        to = message((s // 2 - z + 4) % 4, core) * 64
        goes = goes + both[s : s + 1] * (to + before[s : s + 1])
        source = message((z - s // 2 + 4) % 4, core) * 64
        value = source + before[DP + s : DP + s + 1]
        comes = comes + jnp.where(new_mine == old[s : s + 1, :], value, 0)
    comes = jnp.sum(comes, axis=1, keepdims=True)

    def places(code):
        k, rank = code >> 6, code & 63
        main = jnp.where(rank < MAIN, k * MAIN + rank, -1)
        return main, jnp.where(rank < MAIN, -1, k * 2 * REST + rank - MAIN)

    def onehot(equal):
        return equal.astype(jnp.float32).astype(jnp.bfloat16)

    def index(shape, axis):
        return lax.broadcasted_iota(jnp.int32, shape, axis)

    main, rest = places(goes)
    pack[...] = onehot(index((DP * MAIN, ROWS), 0) == main)
    rest = jnp.concatenate([rest, jnp.where(rest < 0, rest, rest + REST)], axis=1)
    pack_rest[...] = onehot(index((DP * 2 * REST, 2 * ROWS), 0) == rest)
    main, rest = places(comes)
    take[...] = onehot(index((ROWS, DP * MAIN), 1) == main)
    rest = jnp.concatenate([rest, jnp.where(rest < 0, rest, rest + REST)], axis=0)
    take_rest[...] = onehot(index((2 * ROWS, DP * 2 * REST), 1) == rest)


def row_plan(old_rows, new_rows):
    place = lax.axis_index("dp").astype(jnp.int32).reshape(1)
    shapes = [
        (DP * MAIN, ROWS),
        (DP * 2 * REST, 2 * ROWS),
        (ROWS, DP * MAIN),
        (2 * ROWS, DP * 2 * REST),
    ]
    plan = call(
        row_plan_kernel,
        "row_plan",
        [SMEM, VMEM, VMEM],
        [VMEM] * 4,
        [jax.ShapeDtypeStruct(shape, jnp.bfloat16) for shape in shapes],
        [],
        1,
        place,
        old_rows,
        new_rows,
    )
    return plan[:2], plan[2:]


def unit_plan_kernel(place, units, send, take):
    m = place[0]
    lane = lax.broadcasted_iota(jnp.int32, (1, UNIT), 1)
    line = lax.broadcasted_iota(jnp.int32, (UNITS, 1), 0)
    earlier = line < lane

    to_row = jnp.zeros((UNITS, UNIT), jnp.int32)
    to_column = jnp.zeros((UNITS, UNITS), jnp.int32)
    for t in range(1, MP):
        to_row = to_row + jnp.where(turned(units[t : t + 1, :]) == m * UNITS + lane, t, 0)
        to_column = to_column + jnp.where(units[t : t + 1, :] == m * UNITS + line, t, 0)
    to_row = jnp.sum(to_row, axis=0, keepdims=True)
    to_column = jnp.sum(to_column, axis=1, keepdims=True)
    rank = jnp.sum(((to_row == to_column) & earlier).astype(jnp.int32), axis=0, keepdims=True)
    send[...] = to_row * PAIR + rank

    row = units[pl.ds(m, 1), :]
    column = turned(row)
    from_row, from_column = jnp.zeros_like(row), jnp.zeros_like(column)
    for t in range(1, MP):
        from_row = from_row + (row >= t * UNITS).astype(jnp.int32)
        from_column = from_column + (column >= t * UNITS).astype(jnp.int32)
    lower = (from_row == from_column) & (column < row)
    take[...] = from_row * PAIR + jnp.sum(lower.astype(jnp.int32), axis=0, keepdims=True)


def unit_plan(new_units):
    place = lax.axis_index("mp").astype(jnp.int32).reshape(1)
    return call(
        unit_plan_kernel,
        "unit_plan",
        [SMEM, VMEM],
        [VMEM] * 2,
        [jax.ShapeDtypeStruct((1, n), jnp.int32) for n in (UNIT, UNITS)],
        [],
        1,
        place,
        new_units,
    )


TERMS = 3


def terms(values):
    split = []
    for _ in range(TERMS):
        split.append(values.astype(jnp.bfloat16))
        values = values - split[-1].astype(jnp.float32)
    return split


def select_rows(onehot, split):
    dot = functools.partial(jnp.dot, preferred_element_type=jnp.float32)
    return functools.reduce(lambda a, b: a + b, [dot(onehot, term) for term in split])


def columns_of(u):
    return slice(u * UNIT, (u + 1) * UNIT)


def swapped(x):
    return pltpu.roll(x, HALF, 1)


def left_lanes(rows):
    return lax.broadcasted_iota(jnp.int32, (rows, UNIT), 1) < HALF


def folded(x, upper):
    first, last = x[:FOLD], x[FOLD:]
    if upper:
        return jnp.where(left_lanes(FOLD), swapped(first), last)
    return jnp.where(left_lanes(FOLD), first, swapped(last))


def unfolded(y, upper):
    if upper:
        return jnp.concatenate([swapped(y), y], axis=0)
    return jnp.concatenate([y, swapped(y)], axis=0)


def joined(values, axis):
    return jnp.concatenate(values, axis=axis)


def pack_rows(tile, pack, pack_rest, outs):
    width = CHUNK * UNIT
    for i in range(0, TILES // 2, CHUNK):
        left = terms(joined([tile(n) for n in range(i, i + CHUNK)], 1))
        right = terms(joined([tile(TILES // 2 + n) for n in range(i, i + CHUNK)], 1))
        main = select_rows(pack[...], [joined(both, 1) for both in zip(left, right)])
        rest = select_rows(pack_rest[...], [joined(both, 0) for both in zip(left, right)])
        columns = slice(i * UNIT, (i + CHUNK) * UNIT)
        for k, out in enumerate(outs):
            rows = slice(k * MAIN, (k + 1) * MAIN)
            out[:MAIN, columns] = main[rows, :width]
            out[MAIN : 2 * MAIN, columns] = main[rows, width:]
            out[2 * MAIN :, columns] = rest[k * 2 * REST : (k + 1) * 2 * REST]


def take_rows(parts, take, take_rest, put):
    width = CHUNK * UNIT
    for i in range(0, TILES // 2, CHUNK):
        columns = slice(i * UNIT, (i + CHUNK) * UNIT)
        left = joined([p[:MAIN, columns] for p in parts], 0)
        right = joined([p[MAIN : 2 * MAIN, columns] for p in parts], 0)
        rest = joined([p[2 * MAIN :, columns] for p in parts], 0)
        main = select_rows(take[...], terms(joined([left, right], 1)))
        rest = select_rows(take_rest[...], terms(rest))
        left, right = main[:, :width] + rest[:ROWS], main[:, width:] + rest[ROWS:]
        for k in range(CHUNK):
            put(i + k, left[:, columns_of(k)])
            put(TILES // 2 + i + k, right[:, columns_of(k)])


class Copies:
    def __init__(self, sems):
        self.sems, self.waiting = sems, []

    def start(self, source, target):
        copy = pltpu.make_async_copy(source, target, self.sems.at[len(self.waiting)])
        copy.start()
        self.waiting.append(copy)
        return copy

    def wait(self):
        for copy in self.waiting:
            copy.wait()


PARTS = 3
SPAN = UNITS // PARTS


def span_of(i):
    return slice(i * SPAN * UNIT, (i + 1) * SPAN * UNIT)


class Loads:
    def __init__(self, sems):
        self.sems, self.arrays = sems, []

    def start(self, *pairs):
        parts = [[] for _ in pairs]
        for i in range(PARTS):
            for k, (source, target) in enumerate(pairs):
                sem = self.sems.at[(len(self.arrays) + k) * PARTS + i]
                copy = pltpu.make_async_copy(
                    source.at[:, span_of(i)], target.at[:, span_of(i)], sem
                )
                copy.start()
                parts[k].append(copy)
        self.arrays += parts

    def wait(self, array, unit):
        parts = self.arrays[array]
        for i in range(unit // SPAN + 1):
            if parts[i] is not None:
                parts[i].wait()
                parts[i] = None


MESSAGES = [f32(MESSAGE, WIDE)] * DP
SLOT_ARRAY = pltpu.HBM((SLOTS, BLOCK, UNIT), jnp.float32)
SLOT_SPEC = HBM
ARRAY = pltpu.VMEM((ROWS, COLS), jnp.float32)
FOLDS = pltpu.VMEM((UNITS, FOLD, UNIT), jnp.float32)
HELD = pltpu.VMEM((UNITS, ROWS, UNIT), jnp.float32)


def dma(n):
    return pltpu.SemaphoreType.DMA((n,))


def unit_pack_kernel(send, whole, half, out, whole_here, half_here, folds, loads, stores):
    loads, stores = Loads(loads), Copies(stores)
    loads.start((whole, whole_here), (half, half_here))
    for u in range(UNITS):
        loads.wait(0, u)
        stores.start(whole_here.at[:, columns_of(u)], out.at[send[0, u], pl.ds(0, ROWS)])
        loads.wait(1, u)
        folds[u] = folded(half_here[:, columns_of(u)], True)
        stores.start(folds.at[u], out.at[send[0, u], pl.ds(ROWS, FOLD)])
    stores.wait()


def unit_pack(whole, half, send):
    return call(
        unit_pack_kernel,
        "unit_pack",
        [SMEM, HBM, HBM],
        SLOT_SPEC,
        SLOT_ARRAY,
        [ARRAY, ARRAY, FOLDS, dma(2 * PARTS), dma(2 * UNITS)],
        9,
        send,
        whole,
        half,
    )


def row_pack_kernel(pack, pack_rest, whole, half, *rest):
    outs, (whole_here, half_here, loads) = rest[:DP], rest[DP:]
    loads = Loads(loads)
    loads.start((whole, whole_here), (half, half_here))

    def unit(k, u):
        u = min(u, UNITS - 1)
        loads.wait(k, u)
        return (whole_here, half_here)[k][:, columns_of(u)]

    def tile(n):
        if n < UNITS:
            return unit(0, n)
        u = 2 * (n - UNITS)
        return jnp.where(left_lanes(ROWS), unit(1, u), swapped(unit(1, u + 1)))

    pack_rows(tile, pack, pack_rest, outs)


def row_pack(whole, half, pack):
    return call(
        row_pack_kernel,
        "row_pack",
        [VMEM, VMEM, HBM, HBM],
        [VMEM] * DP,
        MESSAGES,
        [ARRAY, ARRAY, dma(2 * PARTS)],
        9,
        *pack,
        whole,
        half,
    )


def unit_row_pack_kernel(take, pack, pack_rest, recv, *rest):
    outs, (here, sems) = rest[:DP], rest[DP:]
    copies, arriving = Copies(sems), {}
    for i in range(0, TILES // 2, CHUNK):
        for n in [*range(i, i + CHUNK), *range(TILES // 2 + i, TILES // 2 + i + CHUNK)]:
            if n < UNITS:
                arriving[n] = copies.start(recv.at[take[0, n]], here.at[n])

    def unit(u):
        if u in arriving:
            arriving.pop(u).wait()
        return here.at[u]

    def tile(n):
        if n < UNITS:
            return unit(n)[:ROWS]
        u = 2 * (n - UNITS)
        a = unfolded(unit(u)[ROWS:], False)
        b = unfolded(unit(min(u + 1, UNITS - 1))[ROWS:], True)
        return jnp.where(left_lanes(ROWS), a, b)

    pack_rows(tile, pack, pack_rest, outs)


def unit_row_pack(recv, take, pack):
    return call(
        unit_row_pack_kernel,
        "unit_row_pack",
        [SMEM, VMEM, VMEM, ANY],
        [VMEM] * DP,
        MESSAGES,
        [pltpu.VMEM((UNITS, BLOCK, UNIT), jnp.float32), dma(UNITS)],
        10,
        take,
        *pack,
        recv,
    )


def row_unit_pack_kernel(send, take, take_rest, *rest):
    parts, (out, held, folds, sems) = rest[:DP], rest[DP:]
    copies = Copies(sems)

    def put(n, tile):
        if n < UNITS:
            held[n] = tile
            copies.start(held.at[n], out.at[send[0, n], pl.ds(0, ROWS)])
            return
        for u, upper in ((2 * (n - UNITS), False), (2 * (n - UNITS) + 1, True)):
            if u < UNITS:
                folds[u] = folded(tile, upper)
                copies.start(folds.at[u], out.at[send[0, u], pl.ds(ROWS, FOLD)])

    take_rows(parts, take, take_rest, put)
    copies.wait()


def row_unit_pack(parts, send, take):
    return call(
        row_unit_pack_kernel,
        "row_unit_pack",
        [SMEM] + [VMEM] * (2 + DP),
        SLOT_SPEC,
        SLOT_ARRAY,
        [HELD, FOLDS, dma(2 * UNITS)],
        10,
        send,
        *take,
        *parts,
    )


def first_kernel(gradient, take, take_rest, *rest):
    parts, (first, half, held, half_held, sems) = rest[:DP], rest[DP:]
    copies, done = Copies(sems), set()

    def put(n, tile):
        if n < UNITS:
            columns = columns_of(n)
            moment = beta_one * tile + (1.0 - beta_one) * gradient[:, columns]
            held[:, columns] = moment
            done.add(n)
            span = n // SPAN
            if all(u in done for u in range(span * SPAN, (span + 1) * SPAN)):
                copies.start(held.at[:, span_of(span)], first.at[:, span_of(span)])
        else:
            half_held[n - UNITS] = tile
            copies.start(half_held.at[n - UNITS], half.at[n - UNITS])

    take_rows(parts, take, take_rest, put)
    copies.wait()


def first_moment(parts, take, gradient):
    return call(
        first_kernel,
        "first_moment",
        [VMEM] * (3 + DP),
        [HBM, HBM],
        [pltpu.HBM((ROWS, COLS), jnp.float32), pltpu.HBM((PAIRS, ROWS, UNIT), jnp.float32)],
        [ARRAY, pltpu.VMEM((PAIRS, ROWS, UNIT), jnp.float32), dma(TILES)],
        11,
        gradient,
        *take,
        *parts,
    )


def update_kernel(take, fixes, recv, first, half, gradient, *rest):
    outs, helds, rest = rest[:3], rest[3:6], rest[6:]
    here, first_here, half_here, gradient_here, whole_loads, unit_loads, stores = rest
    loads, whole, stores = Copies(unit_loads), Loads(whole_loads), Copies(stores)
    arrivals = [loads.start(recv.at[take[0, u]], here.at[u]) for u in range(UNITS // 3)]
    whole.start((gradient, gradient_here), (first, first_here))
    halves = loads.start(half, half_here)
    arrivals += [loads.start(recv.at[take[0, u]], here.at[u]) for u in range(UNITS // 3, UNITS)]
    for u in range(UNITS):
        arrivals[u].wait()
        columns = columns_of(u)
        weight = here[u, :ROWS]
        lower = unfolded(here[u, ROWS:], False)
        if u == 0:
            halves.wait()
        upper = half_here[u // 2]
        if u % 2 == 0:
            upper = swapped(upper)
        second = jnp.where(left_lanes(ROWS), lower, upper)
        whole.wait(0, u)
        g = gradient_here[:, columns]
        second = beta_two * second + (1.0 - beta_two) * g * g
        root = jnp.sqrt(second / fixes[1]) + epsilon
        whole.wait(1, u)
        update = first_here[:, columns] / fixes[0] / root + decay_rate * weight
        for held, out, value in zip(helds, outs, (weight - learn_rate * update, second, update)):
            held[:, columns] = value
            if u % SPAN == SPAN - 1:
                span = span_of(u // SPAN)
                stores.start(held.at[:, span], out.at[:, span])
    stores.wait()


def weight_update(recv, take, fixes, first, half, gradient):
    return call(
        update_kernel,
        "weight_update",
        [SMEM, SMEM, ANY] + [HBM] * 3,
        [HBM] * 3,
        [f32(ROWS, COLS)] * 3,
        [ARRAY] * 3
        + [
            pltpu.VMEM((UNITS, BLOCK, UNIT), jnp.float32),
            ARRAY,
            pltpu.VMEM((PAIRS, ROWS, UNIT), jnp.float32),
            ARRAY,
            dma(2 * PARTS),
            dma(UNITS + 1),
            dma(3 * PARTS),
        ],
        16,
        take,
        fixes,
        recv,
        first,
        half,
        gradient,
    )


def swap_rows(parts):
    arrived = []
    for part, (dz, dc) in zip(parts, MOVES):
        pairs = [(z * 2 + c, (z + dz) % 4 * 2 + (c + dc) % 2) for z in range(4) for c in range(2)]
        arrived.append(lax.ppermute(part, "dp", pairs) if dz or dc else part)
    return arrived


def swap_units(packed):
    packed = packed.reshape(MP, PAIR, BLOCK, UNIT)
    arrived = lax.all_to_all(packed, "mp", split_axis=0, concat_axis=0, tiled=True)
    return arrived.reshape(SLOTS, BLOCK, UNIT)


def body(old_weight, old_first, old_second, gradient, old_rows, new_rows, new_units, step):
    send, take_units = unit_plan(new_units)
    pack, take = row_plan(old_rows, new_rows)
    in_hbm = functools.partial(pltpu.with_memory_space_constraint, memory_space=pltpu.HBM)
    count = step[0].astype(jnp.float32)
    fixes = jnp.stack(
        [
            1.0 - jnp.power(jnp.float32(beta_one), count),
            1.0 - jnp.power(jnp.float32(beta_two), count),
        ]
    )

    units = swap_units(unit_pack(in_hbm(old_first), in_hbm(old_second), send))
    rows = swap_rows(row_pack(in_hbm(old_weight), in_hbm(old_second), pack))
    packed = row_unit_pack(rows, send, take)
    units, packed = lax.optimization_barrier((units, packed))

    units_two = swap_units(packed)
    rows_two = swap_rows(unit_row_pack(units, take_units, pack))

    new_first, half = first_moment(rows_two, take, gradient)
    new_weight, new_second, update = weight_update(
        units_two, take_units, fixes, in_hbm(new_first), in_hbm(half), in_hbm(gradient)
    )
    return new_weight, new_first, new_second, update


def solution(mesh):
    return jax.shard_map(
        body,
        mesh=mesh,
        in_specs=(P("dp", "mp"), P("dp", "mp"), P("dp", "mp"), P("dp", "mp"), P(), P(), P(), P()),
        out_specs=(P("dp", "mp"), P("dp", "mp"), P("dp", "mp"), P("dp", "mp")),
        check_vma=False,
    )
```

```python
import functools

import jax
import jax.numpy as jnp
from jax import lax
from jax.experimental import pallas as pl
from jax.experimental.pallas import tpu as pltpu
from jax.sharding import PartitionSpec as P

UNIT = 128
HALF = UNIT // 2
ROWS = 192
FOLD = ROWS // 2
UNITS = 21
COLS = UNIT * UNITS
DP = 8
MP = 16
ROOM = 36
PAIR = 2
SLOTS = MP * PAIR
BLOCK = ROWS + FOLD
TILES = 32
WIDE = TILES // 2 * UNIT
MAIN = 32
REST = ROOM - MAIN
MESSAGE = 2 * ROOM
PAIRS = TILES - UNITS
CHUNK = 4
VMEM_LIMIT = 24 * 1024 * 1024

beta_one = 0.9
beta_two = 0.999
epsilon = 1e-08
learn_rate = 0.001
decay_rate = 0.1

MOVES = [(0, 0), (0, 1), (1, 0), (3, 0), (1, 1), (3, 1), (2, 0), (2, 1)]
SINGLE = 6
HBM = pl.BlockSpec(memory_space=pltpu.HBM)
ANY = pl.BlockSpec(memory_space=pl.ANY)
VMEM = pl.BlockSpec(memory_space=pltpu.VMEM)
SMEM = pl.BlockSpec(memory_space=pltpu.SMEM)


def f32(*shape):
    return jax.ShapeDtypeStruct(shape, jnp.float32)


def call(kernel, name, ins, outs, out_shape, scratch, mebibytes, *args):
    return pl.pallas_call(
        kernel,
        out_shape=out_shape,
        in_specs=ins,
        out_specs=outs,
        scratch_shapes=scratch,
        compiler_params=pltpu.CompilerParams(vmem_limit_bytes=VMEM_LIMIT),
        cost_estimate=pl.CostEstimate(
            flops=0, bytes_accessed=mebibytes * 2**20, transcendentals=0
        ),
        name=name,
    )(*args)


GRID_ORDER = [(a - x) % 4 * 4 + x for a in range(4) for x in range(4)]


def turned(row):
    n = row.shape[1]
    here = lax.broadcasted_iota(jnp.int32, (n, n), 0)
    there = lax.broadcasted_iota(jnp.int32, (n, n), 1)
    return jnp.sum(jnp.where(here == there, row, 0), axis=1, keepdims=True)


def row_plan_kernel(place, old, new, pack, pack_rest, take, take_rest):
    d = place[0]
    z, c = d // 2, d % 2
    old_mine = old[pl.ds(d, 1), :]
    new_mine = turned(new[pl.ds(d, 1), :])
    here = lax.broadcasted_iota(jnp.int32, (ROWS, ROWS), 0)
    there = lax.broadcasted_iota(jnp.int32, (ROWS, ROWS), 1)
    earlier = (here < there).astype(jnp.float32).astype(jnp.bfloat16)

    goes, comes = [], []
    for s in range(DP):
        hit = (turned(new[s : s + 1, :]) == old_mine).astype(jnp.float32)
        goes.append(jnp.max(hit, axis=0, keepdims=True))
        hit = (new_mine == old[s : s + 1, :]).astype(jnp.float32)
        comes.append(jnp.max(hit, axis=0, keepdims=True))
    both = jnp.concatenate(goes + comes, axis=0)
    before = jnp.dot(both.astype(jnp.bfloat16), earlier, preferred_element_type=jnp.float32)
    both = both.astype(jnp.int32)
    before = before.astype(jnp.int32)

    def message(dz, dc):
        at = 0
        for k, move in enumerate(MOVES):
            at = jnp.where((dz == move[0]) & (dc == move[1]), k, at)
        return at

    goes = jnp.zeros((1, ROWS), jnp.int32)
    comes = jnp.zeros((ROWS, ROWS), jnp.int32)
    for s in range(DP):
        core = (s % 2 + c) % 2
        to = message((s // 2 - z + 4) % 4, core) * 64
        goes = goes + both[s : s + 1] * (to + before[s : s + 1])
        source = message((z - s // 2 + 4) % 4, core) * 64
        value = source + before[DP + s : DP + s + 1]
        comes = comes + jnp.where(new_mine == old[s : s + 1, :], value, 0)
    comes = jnp.sum(comes, axis=1, keepdims=True)

    def places(code):
        k, rank = code >> 6, code & 63
        main = jnp.where(rank < MAIN, k * MAIN + rank, -1)
        return main, jnp.where(rank < MAIN, -1, k * 2 * REST + rank - MAIN)

    def onehot(equal):
        return equal.astype(jnp.float32).astype(jnp.bfloat16)

    def index(shape, axis):
        return lax.broadcasted_iota(jnp.int32, shape, axis)

    main, rest = places(goes)
    pack[...] = onehot(index((DP * MAIN, ROWS), 0) == main)
    rest = jnp.concatenate([rest, jnp.where(rest < 0, rest, rest + REST)], axis=1)
    pack_rest[...] = onehot(index((DP * 2 * REST, 2 * ROWS), 0) == rest)
    main, rest = places(comes)
    take[...] = onehot(index((ROWS, DP * MAIN), 1) == main)
    rest = jnp.concatenate([rest, jnp.where(rest < 0, rest, rest + REST)], axis=0)
    take_rest[...] = onehot(index((2 * ROWS, DP * 2 * REST), 1) == rest)


def row_plan(old_rows, new_rows):
    place = lax.axis_index("dp").astype(jnp.int32).reshape(1)
    shapes = [
        (DP * MAIN, ROWS),
        (DP * 2 * REST, 2 * ROWS),
        (ROWS, DP * MAIN),
        (2 * ROWS, DP * 2 * REST),
    ]
    plan = call(
        row_plan_kernel,
        "row_plan",
        [SMEM, VMEM, VMEM],
        [VMEM] * 4,
        [jax.ShapeDtypeStruct(shape, jnp.bfloat16) for shape in shapes],
        [],
        1,
        place,
        old_rows,
        new_rows,
    )
    return plan[:2], plan[2:]


def chunk_of(shard):
    return ((shard >> 2) + shard & 3) * 4 + (shard & 3)


def unit_plan_kernel(place, units, send, take):
    m = place[0]
    lane = lax.broadcasted_iota(jnp.int32, (1, UNIT), 1)
    line = lax.broadcasted_iota(jnp.int32, (UNITS, 1), 0)
    earlier = line < lane

    to_row = jnp.zeros((UNITS, UNIT), jnp.int32)
    to_column = jnp.zeros((UNITS, UNITS), jnp.int32)
    for t in range(1, MP):
        to_row = to_row + jnp.where(turned(units[t : t + 1, :]) == m * UNITS + lane, t, 0)
        to_column = to_column + jnp.where(units[t : t + 1, :] == m * UNITS + line, t, 0)
    to_row = jnp.sum(to_row, axis=0, keepdims=True)
    to_column = jnp.sum(to_column, axis=1, keepdims=True)
    rank = jnp.sum(((to_row == to_column) & earlier).astype(jnp.int32), axis=0, keepdims=True)
    send[...] = chunk_of(to_row) * PAIR + rank

    row = units[pl.ds(m, 1), :]
    column = turned(row)
    from_row, from_column = jnp.zeros_like(row), jnp.zeros_like(column)
    for t in range(1, MP):
        from_row = from_row + (row >= t * UNITS).astype(jnp.int32)
        from_column = from_column + (column >= t * UNITS).astype(jnp.int32)
    lower = (from_row == from_column) & (column < row)
    take[...] = chunk_of(from_row) * PAIR + jnp.sum(lower.astype(jnp.int32), axis=0, keepdims=True)


def unit_plan(new_units):
    place = lax.axis_index("mp").astype(jnp.int32).reshape(1)
    return call(
        unit_plan_kernel,
        "unit_plan",
        [SMEM, VMEM],
        [VMEM] * 2,
        [jax.ShapeDtypeStruct((1, n), jnp.int32) for n in (UNIT, UNITS)],
        [],
        1,
        place,
        new_units,
    )


TERMS = 2


def terms(values):
    split = []
    for _ in range(TERMS):
        split.append(values.astype(jnp.bfloat16))
        values = values - split[-1].astype(jnp.float32)
    return split


def select_rows(onehot, split):
    dot = functools.partial(jnp.dot, preferred_element_type=jnp.float32)
    return functools.reduce(lambda a, b: a + b, [dot(onehot, term) for term in split])


def columns_of(u):
    return slice(u * UNIT, (u + 1) * UNIT)


def swapped(x):
    return pltpu.roll(x, HALF, 1)


def left_lanes(rows):
    return lax.broadcasted_iota(jnp.int32, (rows, UNIT), 1) < HALF


def folded(x, upper):
    first, last = x[:FOLD], x[FOLD:]
    if upper:
        return jnp.where(left_lanes(FOLD), swapped(first), last)
    return jnp.where(left_lanes(FOLD), first, swapped(last))


def unfolded(y, upper):
    if upper:
        return jnp.concatenate([swapped(y), y], axis=0)
    return jnp.concatenate([y, swapped(y)], axis=0)


def joined(values, axis):
    return jnp.concatenate(values, axis=axis)


def pack_rows(tile, pack, pack_rest, outs):
    double = outs[SINGLE]
    outs = [*outs[:SINGLE], double.at[pl.ds(0, MESSAGE)], double.at[pl.ds(MESSAGE, MESSAGE)]]
    width = CHUNK * UNIT
    for i in range(0, TILES // 2, CHUNK):
        left = terms(joined([tile(n) for n in range(i, i + CHUNK)], 1))
        right = terms(joined([tile(TILES // 2 + n) for n in range(i, i + CHUNK)], 1))
        main = select_rows(pack[...], [joined(both, 1) for both in zip(left, right)])
        rest = select_rows(pack_rest[...], [joined(both, 0) for both in zip(left, right)])
        columns = slice(i * UNIT, (i + CHUNK) * UNIT)
        for k, out in enumerate(outs):
            rows = slice(k * MAIN, (k + 1) * MAIN)
            out[:MAIN, columns] = main[rows, :width]
            out[MAIN : 2 * MAIN, columns] = main[rows, width:]
            out[2 * MAIN :, columns] = rest[k * 2 * REST : (k + 1) * 2 * REST]


def take_rows(parts, take, take_rest, put):
    parts = [*parts[:SINGLE], parts[SINGLE].at[pl.ds(0, MESSAGE)], parts[SINGLE + 1]]
    width = CHUNK * UNIT
    for i in range(0, TILES // 2, CHUNK):
        columns = slice(i * UNIT, (i + CHUNK) * UNIT)
        left = joined([p[:MAIN, columns] for p in parts], 0)
        right = joined([p[MAIN : 2 * MAIN, columns] for p in parts], 0)
        rest = joined([p[2 * MAIN :, columns] for p in parts], 0)
        main = select_rows(take[...], terms(joined([left, right], 1)))
        rest = select_rows(take_rest[...], terms(rest))
        left, right = main[:, :width] + rest[:ROWS], main[:, width:] + rest[ROWS:]
        for k in range(CHUNK):
            put(i + k, left[:, columns_of(k)])
            put(TILES // 2 + i + k, right[:, columns_of(k)])


class Copies:
    def __init__(self, sems):
        self.sems, self.waiting = sems, []

    def start(self, source, target):
        copy = pltpu.make_async_copy(source, target, self.sems.at[len(self.waiting)])
        copy.start()
        self.waiting.append(copy)
        return copy

    def wait(self):
        for copy in self.waiting:
            copy.wait()


PARTS = 7
SPAN = UNITS // PARTS


def span_of(i):
    return slice(i * SPAN * UNIT, (i + 1) * SPAN * UNIT)


class Loads:
    def __init__(self, sems):
        self.sems, self.arrays = sems, []

    def start(self, *pairs):
        parts = [[] for _ in pairs]
        for i in range(PARTS):
            for k, (source, target) in enumerate(pairs):
                sem = self.sems.at[(len(self.arrays) + k) * PARTS + i]
                copy = pltpu.make_async_copy(
                    source.at[:, span_of(i)], target.at[:, span_of(i)], sem
                )
                copy.start()
                parts[k].append(copy)
        self.arrays += parts

    def wait(self, array, unit):
        parts = self.arrays[array]
        for i in range(unit // SPAN + 1):
            if parts[i] is not None:
                parts[i].wait()
                parts[i] = None


MESSAGES = [f32(MESSAGE, WIDE)] * SINGLE + [f32(2 * MESSAGE, WIDE)]
N_OUT = len(MESSAGES)
SLOT_ARRAY = pltpu.HBM((SLOTS, BLOCK, UNIT), jnp.float32)
SLOT_SPEC = HBM
ARRAY = pltpu.VMEM((ROWS, COLS), jnp.float32)
FOLDS = pltpu.VMEM((UNITS, FOLD, UNIT), jnp.float32)
HELD = pltpu.VMEM((UNITS, ROWS, UNIT), jnp.float32)


def dma(n):
    return pltpu.SemaphoreType.DMA((n,))


def unit_pack_kernel(send, whole, half, out, whole_here, half_here, folds, loads, stores):
    loads, stores = Loads(loads), Copies(stores)
    loads.start((whole, whole_here), (half, half_here))
    for u in range(UNITS):
        loads.wait(0, u)
        stores.start(whole_here.at[:, columns_of(u)], out.at[send[0, u], pl.ds(0, ROWS)])
        loads.wait(1, u)
        folds[u] = folded(half_here[:, columns_of(u)], True)
        stores.start(folds.at[u], out.at[send[0, u], pl.ds(ROWS, FOLD)])
    stores.wait()


def unit_pack(whole, half, send):
    return call(
        unit_pack_kernel,
        "unit_pack",
        [SMEM, HBM, HBM],
        SLOT_SPEC,
        SLOT_ARRAY,
        [ARRAY, ARRAY, FOLDS, dma(2 * PARTS), dma(2 * UNITS)],
        9,
        send,
        whole,
        half,
    )


def row_pack_kernel(pack, pack_rest, whole, half, *rest):
    outs, (whole_here, half_here, loads) = rest[:N_OUT], rest[N_OUT:]
    loads = Loads(loads)
    loads.start((whole, whole_here), (half, half_here))

    def unit(k, u):
        u = min(u, UNITS - 1)
        loads.wait(k, u)
        return (whole_here, half_here)[k][:, columns_of(u)]

    def tile(n):
        if n < UNITS:
            return unit(0, n)
        u = 2 * (n - UNITS)
        return jnp.where(left_lanes(ROWS), unit(1, u), swapped(unit(1, u + 1)))

    pack_rows(tile, pack, pack_rest, outs)


def row_pack(whole, half, pack):
    return call(
        row_pack_kernel,
        "row_pack",
        [VMEM, VMEM, HBM, HBM],
        [VMEM] * N_OUT,
        MESSAGES,
        [ARRAY, ARRAY, dma(2 * PARTS)],
        9,
        *pack,
        whole,
        half,
    )


def unit_row_pack_kernel(take, pack, pack_rest, recv, *rest):
    outs, (here, sems) = rest[:N_OUT], rest[N_OUT:]
    copies, arriving = Copies(sems), {}
    for i in range(0, TILES // 2, CHUNK):
        for n in [*range(i, i + CHUNK), *range(TILES // 2 + i, TILES // 2 + i + CHUNK)]:
            if n < UNITS:
                arriving[n] = copies.start(recv.at[take[0, n]], here.at[n])

    def unit(u):
        if u in arriving:
            arriving.pop(u).wait()
        return here.at[u]

    def tile(n):
        if n < UNITS:
            return unit(n)[:ROWS]
        u = 2 * (n - UNITS)
        a = unfolded(unit(u)[ROWS:], False)
        b = unfolded(unit(min(u + 1, UNITS - 1))[ROWS:], True)
        return jnp.where(left_lanes(ROWS), a, b)

    pack_rows(tile, pack, pack_rest, outs)


def unit_row_pack(recv, take, pack):
    return call(
        unit_row_pack_kernel,
        "unit_row_pack",
        [SMEM, VMEM, VMEM, ANY],
        [VMEM] * N_OUT,
        MESSAGES,
        [pltpu.VMEM((UNITS, BLOCK, UNIT), jnp.float32), dma(UNITS)],
        10,
        take,
        *pack,
        recv,
    )


def row_unit_pack_kernel(send, take, take_rest, *rest):
    parts, (out, held, folds, sems) = rest[:DP], rest[DP:]
    copies = Copies(sems)

    def put(n, tile):
        if n < UNITS:
            held[n] = tile
            copies.start(held.at[n], out.at[send[0, n], pl.ds(0, ROWS)])
            return
        for u, upper in ((2 * (n - UNITS), False), (2 * (n - UNITS) + 1, True)):
            if u < UNITS:
                folds[u] = folded(tile, upper)
                copies.start(folds.at[u], out.at[send[0, u], pl.ds(ROWS, FOLD)])

    take_rows(parts, take, take_rest, put)
    copies.wait()


def row_unit_pack(parts, send, take):
    return call(
        row_unit_pack_kernel,
        "row_unit_pack",
        [SMEM] + [VMEM] * (2 + DP),
        SLOT_SPEC,
        SLOT_ARRAY,
        [HELD, FOLDS, dma(2 * UNITS)],
        10,
        send,
        *take,
        *parts,
    )


def first_kernel(fixes, gradient, take, take_rest, *rest):
    parts, (first, known, other, held, half, known_held, other_held, sems) = rest[:DP], rest[DP:]
    copies = Copies(sems)

    def put(n, tile):
        if n < UNITS:
            columns = columns_of(n)
            held[:, columns] = beta_one * tile + (1.0 - beta_one) * gradient[:, columns]
        else:
            half[n - UNITS] = tile

    take_rows(parts, take, take_rest, put)
    for u in range(UNITS):
        columns = columns_of(u)
        upper = half[u // 2]
        if u % 2 == 0:
            upper = swapped(upper)
        g = gradient[:, columns]
        added = (1.0 - beta_two) * g * g
        second = beta_two * upper + added
        root = jnp.sqrt(second * fixes[1]) + epsilon
        scaled = held[:, columns] * fixes[0]
        known_held[:, columns] = jnp.where(left_lanes(ROWS), scaled, scaled / root)
        other_held[:, columns] = jnp.where(left_lanes(ROWS), added, second)
        if u % SPAN == SPAN - 1:
            span = span_of(u // SPAN)
            for here, out in ((held, first), (known_held, known), (other_held, other)):
                copies.start(here.at[:, span], out.at[:, span])
    copies.wait()


def first_moment(parts, take, gradient, fixes):
    whole = pltpu.HBM((ROWS, COLS), jnp.float32)
    return call(
        first_kernel,
        "first_moment",
        [SMEM] + [VMEM] * (3 + DP),
        [HBM] * 3,
        [whole] * 3,
        [ARRAY, pltpu.VMEM((PAIRS, ROWS, UNIT), jnp.float32), ARRAY, ARRAY, dma(3 * PARTS)],
        12,
        fixes,
        gradient,
        *take,
        *parts,
    )


def update_kernel(take, fixes, recv, known, other, *rest):
    outs, helds, rest = rest[:3], rest[3:6], rest[6:]
    here, known_here, other_here, whole_loads, unit_loads, stores = rest
    loads, whole, stores = Copies(unit_loads), Loads(whole_loads), Copies(stores)
    arrivals = [loads.start(recv.at[take[0, u]], here.at[u]) for u in range(SPAN)]
    whole.start((other, other_here), (known, known_here))
    arrivals += [loads.start(recv.at[take[0, u]], here.at[u]) for u in range(SPAN, UNITS)]
    for u in range(UNITS):
        arrivals[u].wait()
        whole.wait(0, u)
        whole.wait(1, u)
        columns = columns_of(u)
        weight = here[u, :ROWS]
        lower = unfolded(here[u, ROWS:], False)
        added = other_here[:, columns]
        second = jnp.where(left_lanes(ROWS), beta_two * lower + added, added)
        root = jnp.sqrt(second * fixes[1]) + epsilon
        scaled = known_here[:, columns]
        update = jnp.where(left_lanes(ROWS), scaled / root, scaled) + decay_rate * weight
        for held, out, value in zip(helds, outs, (weight - learn_rate * update, second, update)):
            held[:, columns] = value
            if u % SPAN == SPAN - 1:
                span = span_of(u // SPAN)
                stores.start(held.at[:, span], out.at[:, span])
    stores.wait()


def weight_update(recv, take, fixes, known, other):
    return call(
        update_kernel,
        "weight_update",
        [SMEM, SMEM, ANY] + [HBM] * 2,
        [HBM] * 3,
        [f32(ROWS, COLS)] * 3,
        [ARRAY] * 3
        + [
            pltpu.VMEM((UNITS, BLOCK, UNIT), jnp.float32),
            ARRAY,
            ARRAY,
            dma(2 * PARTS),
            dma(UNITS),
            dma(3 * PARTS),
        ],
        14,
        take,
        fixes,
        recv,
        known,
        other,
    )


def move(part, dz, dc):
    pairs = [(z * 2 + c, (z + dz) % 4 * 2 + (c + dc) % 2) for z in range(4) for c in range(2)]
    return lax.ppermute(part, "dp", pairs)


def swap_rows(parts):
    arrived = [move(part, *step) if any(step) else part for part, step in zip(parts, MOVES)]
    return arrived + [move(arrived[SINGLE][MESSAGE:], 0, 1)]


def swap_units(packed):
    packed = packed.reshape(MP, PAIR, BLOCK, UNIT)
    arrived = lax.all_to_all(
        packed, "mp", split_axis=0, concat_axis=0, tiled=True, axis_index_groups=[GRID_ORDER]
    )
    return arrived.reshape(SLOTS, BLOCK, UNIT)


def body(old_weight, old_first, old_second, gradient, old_rows, new_rows, new_units, step):
    send, take_units = unit_plan(new_units)
    pack, take = row_plan(old_rows, new_rows)
    in_hbm = functools.partial(pltpu.with_memory_space_constraint, memory_space=pltpu.HBM)
    count = step[0].astype(jnp.float32)
    fixes = jnp.stack(
        [
            1.0 / (1.0 - jnp.power(jnp.float32(beta_one), count)),
            1.0 / (1.0 - jnp.power(jnp.float32(beta_two), count)),
        ]
    )

    units = swap_units(unit_pack(in_hbm(old_first), in_hbm(old_second), send))
    rows = swap_rows(row_pack(in_hbm(old_weight), in_hbm(old_second), pack))
    packed = row_unit_pack(rows, send, take)
    units, packed = lax.optimization_barrier((units, packed))

    units_two = swap_units(packed)
    rows_two = swap_rows(unit_row_pack(units, take_units, pack))

    new_first, known, other = first_moment(rows_two, take, gradient, fixes)
    new_weight, new_second, update = weight_update(
        units_two, take_units, fixes, in_hbm(known), in_hbm(other)
    )
    return new_weight, new_first, new_second, update


def solution(mesh):
    return jax.shard_map(
        body,
        mesh=mesh,
        in_specs=(P("dp", "mp"), P("dp", "mp"), P("dp", "mp"), P("dp", "mp"), P(), P(), P(), P()),
        out_specs=(P("dp", "mp"), P("dp", "mp"), P("dp", "mp"), P("dp", "mp")),
        check_vma=False,
    )
```

```python
import functools

import jax
import jax.numpy as jnp
from jax import lax
from jax.experimental import pallas as pl
from jax.experimental.pallas import tpu as pltpu
from jax.sharding import PartitionSpec as P

UNIT = 128
HALF = UNIT // 2
ROWS = 192
FOLD = ROWS // 2
UNITS = 21
COLS = UNIT * UNITS
DP = 8
MP = 16
ROOM = 36
PAIR = 2
SLOTS = MP * PAIR
BLOCK = ROWS + FOLD
TILES = 32
WIDE = TILES // 2 * UNIT
MAIN = 32
REST = ROOM - MAIN
MESSAGE = 2 * ROOM
PAIRS = TILES - UNITS
CHUNK = 4
VMEM_LIMIT = 24 * 1024 * 1024

beta_one = 0.9
beta_two = 0.999
epsilon = 1e-08
learn_rate = 0.001
decay_rate = 0.1

MOVES = [(0, 0), (0, 1), (1, 0), (3, 0), (1, 1), (3, 1), (2, 0), (2, 1)]
SINGLE = 6
HBM = pl.BlockSpec(memory_space=pltpu.HBM)
ANY = pl.BlockSpec(memory_space=pl.ANY)
VMEM = pl.BlockSpec(memory_space=pltpu.VMEM)
SMEM = pl.BlockSpec(memory_space=pltpu.SMEM)


def f32(*shape):
    return jax.ShapeDtypeStruct(shape, jnp.float32)


def call(kernel, name, ins, outs, out_shape, scratch, mebibytes, *args):
    return pl.pallas_call(
        kernel,
        out_shape=out_shape,
        in_specs=ins,
        out_specs=outs,
        scratch_shapes=scratch,
        compiler_params=pltpu.CompilerParams(vmem_limit_bytes=VMEM_LIMIT),
        cost_estimate=pl.CostEstimate(
            flops=0, bytes_accessed=mebibytes * 2**20, transcendentals=0
        ),
        name=name,
    )(*args)


GRID_ORDER = [(x - a) % 4 * 4 + x for a in range(4) for x in range(4)]


def turned(row):
    n = row.shape[1]
    here = lax.broadcasted_iota(jnp.int32, (n, n), 0)
    there = lax.broadcasted_iota(jnp.int32, (n, n), 1)
    return jnp.sum(jnp.where(here == there, row, 0), axis=1, keepdims=True)


def row_plan_kernel(place, old, new, pack, pack_rest, take, take_rest):
    d = place[0]
    z, c = d // 2, d % 2
    old_mine = old[pl.ds(d, 1), :]
    new_mine = turned(new[pl.ds(d, 1), :])
    here = lax.broadcasted_iota(jnp.int32, (ROWS, ROWS), 0)
    there = lax.broadcasted_iota(jnp.int32, (ROWS, ROWS), 1)
    earlier = (here < there).astype(jnp.float32).astype(jnp.bfloat16)

    goes, comes = [], []
    for s in range(DP):
        hit = (turned(new[s : s + 1, :]) == old_mine).astype(jnp.float32)
        goes.append(jnp.max(hit, axis=0, keepdims=True))
        hit = (new_mine == old[s : s + 1, :]).astype(jnp.float32)
        comes.append(jnp.max(hit, axis=0, keepdims=True))
    both = jnp.concatenate(goes + comes, axis=0)
    before = jnp.dot(both.astype(jnp.bfloat16), earlier, preferred_element_type=jnp.float32)
    both = both.astype(jnp.int32)
    before = before.astype(jnp.int32)

    def message(dz, dc):
        at = 0
        for k, move in enumerate(MOVES):
            at = jnp.where((dz == move[0]) & (dc == move[1]), k, at)
        return at

    goes = jnp.zeros((1, ROWS), jnp.int32)
    comes = jnp.zeros((ROWS, ROWS), jnp.int32)
    for s in range(DP):
        core = (s % 2 + c) % 2
        to = message((s // 2 - z + 4) % 4, core) * 64
        goes = goes + both[s : s + 1] * (to + before[s : s + 1])
        source = message((z - s // 2 + 4) % 4, core) * 64
        value = source + before[DP + s : DP + s + 1]
        comes = comes + jnp.where(new_mine == old[s : s + 1, :], value, 0)
    comes = jnp.sum(comes, axis=1, keepdims=True)

    def places(code):
        k, rank = code >> 6, code & 63
        main = jnp.where(rank < MAIN, k * MAIN + rank, -1)
        return main, jnp.where(rank < MAIN, -1, k * 2 * REST + rank - MAIN)

    def onehot(equal):
        return equal.astype(jnp.float32).astype(jnp.bfloat16)

    def index(shape, axis):
        return lax.broadcasted_iota(jnp.int32, shape, axis)

    main, rest = places(goes)
    pack[...] = onehot(index((DP * MAIN, ROWS), 0) == main)
    rest = jnp.concatenate([rest, jnp.where(rest < 0, rest, rest + REST)], axis=1)
    pack_rest[...] = onehot(index((DP * 2 * REST, 2 * ROWS), 0) == rest)
    main, rest = places(comes)
    take[...] = onehot(index((ROWS, DP * MAIN), 1) == main)
    rest = jnp.concatenate([rest, jnp.where(rest < 0, rest, rest + REST)], axis=0)
    take_rest[...] = onehot(index((2 * ROWS, DP * 2 * REST), 1) == rest)


def row_plan(old_rows, new_rows):
    place = lax.axis_index("dp").astype(jnp.int32).reshape(1)
    shapes = [
        (DP * MAIN, ROWS),
        (DP * 2 * REST, 2 * ROWS),
        (ROWS, DP * MAIN),
        (2 * ROWS, DP * 2 * REST),
    ]
    plan = call(
        row_plan_kernel,
        "row_plan",
        [SMEM, VMEM, VMEM],
        [VMEM] * 4,
        [jax.ShapeDtypeStruct(shape, jnp.bfloat16) for shape in shapes],
        [],
        1,
        place,
        old_rows,
        new_rows,
    )
    return plan[:2], plan[2:]


def chunk_of(shard):
    return (shard - (shard >> 2) & 3) * 4 + (shard & 3)


def unit_plan_kernel(place, units, send, take):
    m = place[0]
    lane = lax.broadcasted_iota(jnp.int32, (1, UNIT), 1)
    line = lax.broadcasted_iota(jnp.int32, (UNITS, 1), 0)
    earlier = line < lane

    to_row = jnp.zeros((UNITS, UNIT), jnp.int32)
    to_column = jnp.zeros((UNITS, UNITS), jnp.int32)
    for t in range(1, MP):
        to_row = to_row + jnp.where(turned(units[t : t + 1, :]) == m * UNITS + lane, t, 0)
        to_column = to_column + jnp.where(units[t : t + 1, :] == m * UNITS + line, t, 0)
    to_row = jnp.sum(to_row, axis=0, keepdims=True)
    to_column = jnp.sum(to_column, axis=1, keepdims=True)
    rank = jnp.sum(((to_row == to_column) & earlier).astype(jnp.int32), axis=0, keepdims=True)
    send[...] = chunk_of(to_row) * PAIR + rank

    row = units[pl.ds(m, 1), :]
    column = turned(row)
    from_row, from_column = jnp.zeros_like(row), jnp.zeros_like(column)
    for t in range(1, MP):
        from_row = from_row + (row >= t * UNITS).astype(jnp.int32)
        from_column = from_column + (column >= t * UNITS).astype(jnp.int32)
    lower = (from_row == from_column) & (column < row)
    take[...] = chunk_of(from_row) * PAIR + jnp.sum(lower.astype(jnp.int32), axis=0, keepdims=True)


def unit_plan(new_units):
    place = lax.axis_index("mp").astype(jnp.int32).reshape(1)
    return call(
        unit_plan_kernel,
        "unit_plan",
        [SMEM, VMEM],
        [VMEM] * 2,
        [jax.ShapeDtypeStruct((1, n), jnp.int32) for n in (UNIT, UNITS)],
        [],
        1,
        place,
        new_units,
    )


TERMS = 2


def terms(values):
    split = []
    for _ in range(TERMS):
        split.append(values.astype(jnp.bfloat16))
        values = values - split[-1].astype(jnp.float32)
    return split


def select_rows(onehot, split):
    dot = functools.partial(jnp.dot, preferred_element_type=jnp.float32)
    return functools.reduce(lambda a, b: a + b, [dot(onehot, term) for term in split])


def columns_of(u):
    return slice(u * UNIT, (u + 1) * UNIT)


def swapped(x):
    return pltpu.roll(x, HALF, 1)


def left_lanes(rows):
    return lax.broadcasted_iota(jnp.int32, (rows, UNIT), 1) < HALF


def folded(x, upper):
    first, last = x[:FOLD], x[FOLD:]
    if upper:
        return jnp.where(left_lanes(FOLD), swapped(first), last)
    return jnp.where(left_lanes(FOLD), first, swapped(last))


def unfolded(y, upper):
    if upper:
        return jnp.concatenate([swapped(y), y], axis=0)
    return jnp.concatenate([y, swapped(y)], axis=0)


def joined(values, axis):
    return jnp.concatenate(values, axis=axis)


def pack_rows(tile, pack, pack_rest, outs):
    double = outs[SINGLE]
    outs = [*outs[:SINGLE], double.at[pl.ds(0, MESSAGE)], double.at[pl.ds(MESSAGE, MESSAGE)]]
    width = CHUNK * UNIT
    for i in range(0, TILES // 2, CHUNK):
        left = terms(joined([tile(n) for n in range(i, i + CHUNK)], 1))
        right = terms(joined([tile(TILES // 2 + n) for n in range(i, i + CHUNK)], 1))
        main = select_rows(pack[...], [joined(both, 1) for both in zip(left, right)])
        rest = select_rows(pack_rest[...], [joined(both, 0) for both in zip(left, right)])
        columns = slice(i * UNIT, (i + CHUNK) * UNIT)
        for k, out in enumerate(outs):
            rows = slice(k * MAIN, (k + 1) * MAIN)
            out[:MAIN, columns] = main[rows, :width]
            out[MAIN : 2 * MAIN, columns] = main[rows, width:]
            out[2 * MAIN :, columns] = rest[k * 2 * REST : (k + 1) * 2 * REST]


def take_rows(parts, take, take_rest, put):
    parts = [*parts[:SINGLE], parts[SINGLE].at[pl.ds(0, MESSAGE)], parts[SINGLE + 1]]
    width = CHUNK * UNIT
    for i in range(0, TILES // 2, CHUNK):
        columns = slice(i * UNIT, (i + CHUNK) * UNIT)
        left = joined([p[:MAIN, columns] for p in parts], 0)
        right = joined([p[MAIN : 2 * MAIN, columns] for p in parts], 0)
        rest = joined([p[2 * MAIN :, columns] for p in parts], 0)
        main = select_rows(take[...], terms(joined([left, right], 1)))
        rest = select_rows(take_rest[...], terms(rest))
        left, right = main[:, :width] + rest[:ROWS], main[:, width:] + rest[ROWS:]
        for k in range(CHUNK):
            put(i + k, left[:, columns_of(k)])
            put(TILES // 2 + i + k, right[:, columns_of(k)])


class Copies:
    def __init__(self, sems):
        self.sems, self.waiting = sems, []

    def start(self, source, target):
        copy = pltpu.make_async_copy(source, target, self.sems.at[len(self.waiting)])
        copy.start()
        self.waiting.append(copy)
        return copy

    def wait(self):
        for copy in self.waiting:
            copy.wait()


PARTS = 3
SPAN = UNITS // PARTS


def span_of(i):
    return slice(i * SPAN * UNIT, (i + 1) * SPAN * UNIT)


class Loads:
    def __init__(self, sems):
        self.sems, self.arrays = sems, []

    def start(self, *pairs):
        parts = [[] for _ in pairs]
        for i in range(PARTS):
            for k, (source, target) in enumerate(pairs):
                sem = self.sems.at[(len(self.arrays) + k) * PARTS + i]
                copy = pltpu.make_async_copy(
                    source.at[:, span_of(i)], target.at[:, span_of(i)], sem
                )
                copy.start()
                parts[k].append(copy)
        self.arrays += parts

    def wait(self, array, unit):
        parts = self.arrays[array]
        for i in range(unit // SPAN + 1):
            if parts[i] is not None:
                parts[i].wait()
                parts[i] = None


MESSAGES = [f32(MESSAGE, WIDE)] * SINGLE + [f32(2 * MESSAGE, WIDE)]
N_OUT = len(MESSAGES)
SLOT_ARRAY = pltpu.HBM((SLOTS, BLOCK, UNIT), jnp.float32)
SLOT_SPEC = HBM
ARRAY = pltpu.VMEM((ROWS, COLS), jnp.float32)
FOLDS = pltpu.VMEM((UNITS, FOLD, UNIT), jnp.float32)
HELD = pltpu.VMEM((UNITS, ROWS, UNIT), jnp.float32)


def dma(n):
    return pltpu.SemaphoreType.DMA((n,))


def unit_pack_kernel(send, whole, half, out, whole_here, half_here, folds, loads, stores):
    loads, stores = Loads(loads), Copies(stores)
    loads.start((whole, whole_here), (half, half_here))
    for u in range(UNITS):
        loads.wait(0, u)
        stores.start(whole_here.at[:, columns_of(u)], out.at[send[0, u], pl.ds(0, ROWS)])
        loads.wait(1, u)
        folds[u] = folded(half_here[:, columns_of(u)], True)
        stores.start(folds.at[u], out.at[send[0, u], pl.ds(ROWS, FOLD)])
    stores.wait()


def unit_pack(whole, half, send):
    return call(
        unit_pack_kernel,
        "unit_pack",
        [SMEM, HBM, HBM],
        SLOT_SPEC,
        SLOT_ARRAY,
        [ARRAY, ARRAY, FOLDS, dma(2 * PARTS), dma(2 * UNITS)],
        9,
        send,
        whole,
        half,
    )


def row_pack_kernel(pack, pack_rest, whole, half, *rest):
    outs, (whole_here, half_here, loads) = rest[:N_OUT], rest[N_OUT:]
    loads = Loads(loads)
    loads.start((whole, whole_here), (half, half_here))

    def unit(k, u):
        u = min(u, UNITS - 1)
        loads.wait(k, u)
        return (whole_here, half_here)[k][:, columns_of(u)]

    def tile(n):
        if n < UNITS:
            return unit(0, n)
        u = 2 * (n - UNITS)
        return jnp.where(left_lanes(ROWS), unit(1, u), swapped(unit(1, u + 1)))

    pack_rows(tile, pack, pack_rest, outs)


def row_pack(whole, half, pack):
    return call(
        row_pack_kernel,
        "row_pack",
        [VMEM, VMEM, HBM, HBM],
        [VMEM] * N_OUT,
        MESSAGES,
        [ARRAY, ARRAY, dma(2 * PARTS)],
        9,
        *pack,
        whole,
        half,
    )


def unit_row_pack_kernel(take, pack, pack_rest, recv, *rest):
    outs, (here, sems) = rest[:N_OUT], rest[N_OUT:]
    copies, arriving = Copies(sems), {}
    for i in range(0, TILES // 2, CHUNK):
        for n in [*range(i, i + CHUNK), *range(TILES // 2 + i, TILES // 2 + i + CHUNK)]:
            if n < UNITS:
                arriving[n] = copies.start(recv.at[take[0, n]], here.at[n])

    def unit(u):
        if u in arriving:
            arriving.pop(u).wait()
        return here.at[u]

    def tile(n):
        if n < UNITS:
            return unit(n)[:ROWS]
        u = 2 * (n - UNITS)
        a = unfolded(unit(u)[ROWS:], False)
        b = unfolded(unit(min(u + 1, UNITS - 1))[ROWS:], True)
        return jnp.where(left_lanes(ROWS), a, b)

    pack_rows(tile, pack, pack_rest, outs)


def unit_row_pack(recv, take, pack):
    return call(
        unit_row_pack_kernel,
        "unit_row_pack",
        [SMEM, VMEM, VMEM, ANY],
        [VMEM] * N_OUT,
        MESSAGES,
        [pltpu.VMEM((UNITS, BLOCK, UNIT), jnp.float32), dma(UNITS)],
        10,
        take,
        *pack,
        recv,
    )


def row_unit_pack_kernel(send, take, take_rest, *rest):
    parts, (out, held, folds, sems) = rest[:DP], rest[DP:]
    copies = Copies(sems)

    def put(n, tile):
        if n < UNITS:
            held[n] = tile
            copies.start(held.at[n], out.at[send[0, n], pl.ds(0, ROWS)])
            return
        for u, upper in ((2 * (n - UNITS), False), (2 * (n - UNITS) + 1, True)):
            if u < UNITS:
                folds[u] = folded(tile, upper)
                copies.start(folds.at[u], out.at[send[0, u], pl.ds(ROWS, FOLD)])

    take_rows(parts, take, take_rest, put)
    copies.wait()


def row_unit_pack(parts, send, take):
    return call(
        row_unit_pack_kernel,
        "row_unit_pack",
        [SMEM] + [VMEM] * (2 + DP),
        SLOT_SPEC,
        SLOT_ARRAY,
        [HELD, FOLDS, dma(2 * UNITS)],
        10,
        send,
        *take,
        *parts,
    )


def first_kernel(gradient, take, take_rest, *rest):
    parts, (first, half, held, half_held, sems) = rest[:DP], rest[DP:]
    copies, done = Copies(sems), set()

    def put(n, tile):
        if n < UNITS:
            columns = columns_of(n)
            moment = beta_one * tile + (1.0 - beta_one) * gradient[:, columns]
            held[:, columns] = moment
            done.add(n)
            span = n // SPAN
            if all(u in done for u in range(span * SPAN, (span + 1) * SPAN)):
                copies.start(held.at[:, span_of(span)], first.at[:, span_of(span)])
        else:
            half_held[n - UNITS] = tile
            copies.start(half_held.at[n - UNITS], half.at[n - UNITS])

    take_rows(parts, take, take_rest, put)
    copies.wait()


def first_moment(parts, take, gradient):
    return call(
        first_kernel,
        "first_moment",
        [VMEM] * (3 + DP),
        [HBM, HBM],
        [pltpu.HBM((ROWS, COLS), jnp.float32), pltpu.HBM((PAIRS, ROWS, UNIT), jnp.float32)],
        [ARRAY, pltpu.VMEM((PAIRS, ROWS, UNIT), jnp.float32), dma(TILES)],
        11,
        gradient,
        *take,
        *parts,
    )


def update_kernel(take, fixes, recv, first, half, gradient, *rest):
    outs, helds, rest = rest[:3], rest[3:6], rest[6:]
    here, first_here, half_here, gradient_here, whole_loads, unit_loads, stores = rest
    loads, whole, stores = Copies(unit_loads), Loads(whole_loads), Copies(stores)
    arrivals = [loads.start(recv.at[take[0, u]], here.at[u]) for u in range(UNITS // 3)]
    whole.start((gradient, gradient_here), (first, first_here))
    halves = loads.start(half, half_here)
    arrivals += [loads.start(recv.at[take[0, u]], here.at[u]) for u in range(UNITS // 3, UNITS)]
    for u in range(UNITS):
        arrivals[u].wait()
        columns = columns_of(u)
        weight = here[u, :ROWS]
        lower = unfolded(here[u, ROWS:], False)
        if u == 0:
            halves.wait()
        upper = half_here[u // 2]
        if u % 2 == 0:
            upper = swapped(upper)
        second = jnp.where(left_lanes(ROWS), lower, upper)
        whole.wait(0, u)
        g = gradient_here[:, columns]
        second = beta_two * second + (1.0 - beta_two) * g * g
        root = jnp.sqrt(second / fixes[1]) + epsilon
        whole.wait(1, u)
        update = first_here[:, columns] / fixes[0] / root + decay_rate * weight
        for held, out, value in zip(helds, outs, (weight - learn_rate * update, second, update)):
            held[:, columns] = value
            if u % SPAN == SPAN - 1:
                span = span_of(u // SPAN)
                stores.start(held.at[:, span], out.at[:, span])
    stores.wait()


def weight_update(recv, take, fixes, first, half, gradient):
    return call(
        update_kernel,
        "weight_update",
        [SMEM, SMEM, ANY] + [HBM] * 3,
        [HBM] * 3,
        [f32(ROWS, COLS)] * 3,
        [ARRAY] * 3
        + [
            pltpu.VMEM((UNITS, BLOCK, UNIT), jnp.float32),
            ARRAY,
            pltpu.VMEM((PAIRS, ROWS, UNIT), jnp.float32),
            ARRAY,
            dma(2 * PARTS),
            dma(UNITS + 1),
            dma(3 * PARTS),
        ],
        16,
        take,
        fixes,
        recv,
        first,
        half,
        gradient,
    )


def move(part, dz, dc):
    pairs = [(z * 2 + c, (z + dz) % 4 * 2 + (c + dc) % 2) for z in range(4) for c in range(2)]
    return lax.ppermute(part, "dp", pairs)


def swap_rows(parts):
    arrived = [move(part, *step) if any(step) else part for part, step in zip(parts, MOVES)]
    return arrived + [move(arrived[SINGLE][MESSAGE:], 0, 1)]


def swap_units(packed):
    packed = packed.reshape(MP, PAIR, BLOCK, UNIT)
    arrived = lax.all_to_all(
        packed, "mp", split_axis=0, concat_axis=0, tiled=True, axis_index_groups=[GRID_ORDER]
    )
    return arrived.reshape(SLOTS, BLOCK, UNIT)


def body(old_weight, old_first, old_second, gradient, old_rows, new_rows, new_units, step):
    send, take_units = unit_plan(new_units)
    pack, take = row_plan(old_rows, new_rows)
    in_hbm = functools.partial(pltpu.with_memory_space_constraint, memory_space=pltpu.HBM)
    count = step[0].astype(jnp.float32)
    fixes = jnp.stack(
        [
            1.0 - jnp.power(jnp.float32(beta_one), count),
            1.0 - jnp.power(jnp.float32(beta_two), count),
        ]
    )

    units = swap_units(unit_pack(in_hbm(old_first), in_hbm(old_second), send))
    rows = swap_rows(row_pack(in_hbm(old_weight), in_hbm(old_second), pack))
    packed = row_unit_pack(rows, send, take)
    units, packed = lax.optimization_barrier((units, packed))

    units_two = swap_units(packed)
    rows_two = swap_rows(unit_row_pack(units, take_units, pack))

    new_first, half = first_moment(rows_two, take, gradient)
    new_weight, new_second, update = weight_update(
        units_two, take_units, fixes, in_hbm(new_first), in_hbm(half), in_hbm(gradient)
    )
    return new_weight, new_first, new_second, update


def solution(mesh):
    return jax.shard_map(
        body,
        mesh=mesh,
        in_specs=(P("dp", "mp"), P("dp", "mp"), P("dp", "mp"), P("dp", "mp"), P(), P(), P(), P()),
        out_specs=(P("dp", "mp"), P("dp", "mp"), P("dp", "mp"), P("dp", "mp")),
        check_vma=False,
    )
```

```python
import functools

import jax
import jax.numpy as jnp
from jax import lax
from jax.experimental import pallas as pl
from jax.experimental.pallas import tpu as pltpu
from jax.sharding import PartitionSpec as P

UNIT = 128
HALF = UNIT // 2
ROWS = 192
FOLD = ROWS // 2
UNITS = 21
COLS = UNIT * UNITS
DP = 8
MP = 16
ROOM = 36
PAIR = 2
SLOTS = MP * PAIR
BLOCK = ROWS + FOLD
TILES = 32
WIDE = TILES // 2 * UNIT
MAIN = 32
REST = ROOM - MAIN
MESSAGE = 2 * ROOM
PAIRS = TILES - UNITS
CHUNK = 4
VMEM_LIMIT = 24 * 1024 * 1024

beta_one = 0.9
beta_two = 0.999
epsilon = 1e-08
learn_rate = 0.001
decay_rate = 0.1

MOVES = [(0, 0), (0, 1), (1, 0), (3, 0), (1, 1), (3, 1), (2, 0), (2, 1)]
SINGLE = 6
HBM = pl.BlockSpec(memory_space=pltpu.HBM)
ANY = pl.BlockSpec(memory_space=pl.ANY)
VMEM = pl.BlockSpec(memory_space=pltpu.VMEM)
SMEM = pl.BlockSpec(memory_space=pltpu.SMEM)


def f32(*shape):
    return jax.ShapeDtypeStruct(shape, jnp.float32)


def call(kernel, name, ins, outs, out_shape, scratch, mebibytes, *args):
    return pl.pallas_call(
        kernel,
        out_shape=out_shape,
        in_specs=ins,
        out_specs=outs,
        scratch_shapes=scratch,
        compiler_params=pltpu.CompilerParams(vmem_limit_bytes=VMEM_LIMIT),
        cost_estimate=pl.CostEstimate(
            flops=0, bytes_accessed=mebibytes * 2**20, transcendentals=0
        ),
        name=name,
    )(*args)


GRID_ORDER = [(x - a) % 4 * 4 + x for a in range(4) for x in range(4)]


def turned(row):
    n = row.shape[1]
    here = lax.broadcasted_iota(jnp.int32, (n, n), 0)
    there = lax.broadcasted_iota(jnp.int32, (n, n), 1)
    return jnp.sum(jnp.where(here == there, row, 0), axis=1, keepdims=True)


def row_plan_kernel(place, old, new, pack, pack_rest, take, take_rest):
    d = place[0]
    z, c = d // 2, d % 2
    old_mine = old[pl.ds(d, 1), :]
    new_mine = turned(new[pl.ds(d, 1), :])
    here = lax.broadcasted_iota(jnp.int32, (ROWS, ROWS), 0)
    there = lax.broadcasted_iota(jnp.int32, (ROWS, ROWS), 1)
    earlier = (here < there).astype(jnp.float32).astype(jnp.bfloat16)

    goes, comes = [], []
    for s in range(DP):
        hit = (turned(new[s : s + 1, :]) == old_mine).astype(jnp.float32)
        goes.append(jnp.max(hit, axis=0, keepdims=True))
        hit = (new_mine == old[s : s + 1, :]).astype(jnp.float32)
        comes.append(jnp.max(hit, axis=0, keepdims=True))
    both = jnp.concatenate(goes + comes, axis=0)
    before = jnp.dot(both.astype(jnp.bfloat16), earlier, preferred_element_type=jnp.float32)
    both = both.astype(jnp.int32)
    before = before.astype(jnp.int32)

    def message(dz, dc):
        at = 0
        for k, move in enumerate(MOVES):
            at = jnp.where((dz == move[0]) & (dc == move[1]), k, at)
        return at

    goes = jnp.zeros((1, ROWS), jnp.int32)
    comes = jnp.zeros((ROWS, ROWS), jnp.int32)
    for s in range(DP):
        core = (s % 2 + c) % 2
        to = message((s // 2 - z + 4) % 4, core) * 64
        goes = goes + both[s : s + 1] * (to + before[s : s + 1])
        source = message((z - s // 2 + 4) % 4, core) * 64
        value = source + before[DP + s : DP + s + 1]
        comes = comes + jnp.where(new_mine == old[s : s + 1, :], value, 0)
    comes = jnp.sum(comes, axis=1, keepdims=True)

    def places(code):
        k, rank = code >> 6, code & 63
        main = jnp.where(rank < MAIN, k * MAIN + rank, -1)
        return main, jnp.where(rank < MAIN, -1, k * 2 * REST + rank - MAIN)

    def onehot(equal):
        return equal.astype(jnp.float32).astype(jnp.bfloat16)

    def index(shape, axis):
        return lax.broadcasted_iota(jnp.int32, shape, axis)

    main, rest = places(goes)
    pack[...] = onehot(index((DP * MAIN, ROWS), 0) == main)
    rest = jnp.concatenate([rest, jnp.where(rest < 0, rest, rest + REST)], axis=1)
    pack_rest[...] = onehot(index((DP * 2 * REST, 2 * ROWS), 0) == rest)
    main, rest = places(comes)
    take[...] = onehot(index((ROWS, DP * MAIN), 1) == main)
    rest = jnp.concatenate([rest, jnp.where(rest < 0, rest, rest + REST)], axis=0)
    take_rest[...] = onehot(index((2 * ROWS, DP * 2 * REST), 1) == rest)


def row_plan(old_rows, new_rows):
    place = lax.axis_index("dp").astype(jnp.int32).reshape(1)
    shapes = [
        (DP * MAIN, ROWS),
        (DP * 2 * REST, 2 * ROWS),
        (ROWS, DP * MAIN),
        (2 * ROWS, DP * 2 * REST),
    ]
    plan = call(
        row_plan_kernel,
        "row_plan",
        [SMEM, VMEM, VMEM],
        [VMEM] * 4,
        [jax.ShapeDtypeStruct(shape, jnp.bfloat16) for shape in shapes],
        [],
        1,
        place,
        old_rows,
        new_rows,
    )
    return plan[:2], plan[2:]


def chunk_of(shard):
    return (shard - (shard >> 2) & 3) * 4 + (shard & 3)


def unit_plan_kernel(place, units, send, take):
    m = place[0]
    lane = lax.broadcasted_iota(jnp.int32, (1, UNIT), 1)
    line = lax.broadcasted_iota(jnp.int32, (UNITS, 1), 0)
    earlier = line < lane

    to_row = jnp.zeros((UNITS, UNIT), jnp.int32)
    to_column = jnp.zeros((UNITS, UNITS), jnp.int32)
    for t in range(1, MP):
        to_row = to_row + jnp.where(turned(units[t : t + 1, :]) == m * UNITS + lane, t, 0)
        to_column = to_column + jnp.where(units[t : t + 1, :] == m * UNITS + line, t, 0)
    to_row = jnp.sum(to_row, axis=0, keepdims=True)
    to_column = jnp.sum(to_column, axis=1, keepdims=True)
    rank = jnp.sum(((to_row == to_column) & earlier).astype(jnp.int32), axis=0, keepdims=True)
    send[...] = chunk_of(to_row) * PAIR + rank

    row = units[pl.ds(m, 1), :]
    column = turned(row)
    from_row, from_column = jnp.zeros_like(row), jnp.zeros_like(column)
    for t in range(1, MP):
        from_row = from_row + (row >= t * UNITS).astype(jnp.int32)
        from_column = from_column + (column >= t * UNITS).astype(jnp.int32)
    lower = (from_row == from_column) & (column < row)
    take[...] = chunk_of(from_row) * PAIR + jnp.sum(lower.astype(jnp.int32), axis=0, keepdims=True)


def unit_plan(new_units):
    place = lax.axis_index("mp").astype(jnp.int32).reshape(1)
    return call(
        unit_plan_kernel,
        "unit_plan",
        [SMEM, VMEM],
        [VMEM] * 2,
        [jax.ShapeDtypeStruct((1, n), jnp.int32) for n in (UNIT, UNITS)],
        [],
        1,
        place,
        new_units,
    )


TERMS = 2


def terms(values):
    split = []
    for _ in range(TERMS):
        split.append(values.astype(jnp.bfloat16))
        values = values - split[-1].astype(jnp.float32)
    return split


def select_rows(onehot, split):
    dot = functools.partial(jnp.dot, preferred_element_type=jnp.float32)
    return functools.reduce(lambda a, b: a + b, [dot(onehot, term) for term in split])


def columns_of(u):
    return slice(u * UNIT, (u + 1) * UNIT)


def swapped(x):
    return pltpu.roll(x, HALF, 1)


def left_lanes(rows):
    return lax.broadcasted_iota(jnp.int32, (rows, UNIT), 1) < HALF


def folded(x, upper):
    first, last = x[:FOLD], x[FOLD:]
    if upper:
        return jnp.where(left_lanes(FOLD), swapped(first), last)
    return jnp.where(left_lanes(FOLD), first, swapped(last))


def unfolded(y, upper):
    if upper:
        return jnp.concatenate([swapped(y), y], axis=0)
    return jnp.concatenate([y, swapped(y)], axis=0)


def joined(values, axis):
    return jnp.concatenate(values, axis=axis)


def pack_rows(tile, pack, pack_rest, outs):
    double = outs[SINGLE]
    outs = [*outs[:SINGLE], double.at[pl.ds(0, MESSAGE)], double.at[pl.ds(MESSAGE, MESSAGE)]]
    width = CHUNK * UNIT
    for i in range(0, TILES // 2, CHUNK):
        left = terms(joined([tile(n) for n in range(i, i + CHUNK)], 1))
        right = terms(joined([tile(TILES // 2 + n) for n in range(i, i + CHUNK)], 1))
        main = select_rows(pack[...], [joined(both, 1) for both in zip(left, right)])
        rest = select_rows(pack_rest[...], [joined(both, 0) for both in zip(left, right)])
        columns = slice(i * UNIT, (i + CHUNK) * UNIT)
        for k, out in enumerate(outs):
            rows = slice(k * MAIN, (k + 1) * MAIN)
            out[:MAIN, columns] = main[rows, :width]
            out[MAIN : 2 * MAIN, columns] = main[rows, width:]
            out[2 * MAIN :, columns] = rest[k * 2 * REST : (k + 1) * 2 * REST]


def take_rows(parts, take, take_rest, put):
    parts = [*parts[:SINGLE], parts[SINGLE].at[pl.ds(0, MESSAGE)], parts[SINGLE + 1]]
    width = CHUNK * UNIT
    for i in range(0, TILES // 2, CHUNK):
        columns = slice(i * UNIT, (i + CHUNK) * UNIT)
        left = joined([p[:MAIN, columns] for p in parts], 0)
        right = joined([p[MAIN : 2 * MAIN, columns] for p in parts], 0)
        rest = joined([p[2 * MAIN :, columns] for p in parts], 0)
        main = select_rows(take[...], terms(joined([left, right], 1)))
        rest = select_rows(take_rest[...], terms(rest))
        left, right = main[:, :width] + rest[:ROWS], main[:, width:] + rest[ROWS:]
        for k in range(CHUNK):
            put(i + k, left[:, columns_of(k)])
            put(TILES // 2 + i + k, right[:, columns_of(k)])


class Copies:
    def __init__(self, sems):
        self.sems, self.waiting = sems, []

    def start(self, source, target):
        copy = pltpu.make_async_copy(source, target, self.sems.at[len(self.waiting)])
        copy.start()
        self.waiting.append(copy)
        return copy

    def wait(self):
        for copy in self.waiting:
            copy.wait()


PARTS = 3
SPAN = UNITS // PARTS


def span_of(i):
    return slice(i * SPAN * UNIT, (i + 1) * SPAN * UNIT)


class Loads:
    def __init__(self, sems):
        self.sems, self.arrays = sems, []

    def start(self, *pairs):
        parts = [[] for _ in pairs]
        for i in range(PARTS):
            for k, (source, target) in enumerate(pairs):
                sem = self.sems.at[(len(self.arrays) + k) * PARTS + i]
                copy = pltpu.make_async_copy(
                    source.at[:, span_of(i)], target.at[:, span_of(i)], sem
                )
                copy.start()
                parts[k].append(copy)
        self.arrays += parts

    def wait(self, array, unit):
        parts = self.arrays[array]
        for i in range(unit // SPAN + 1):
            if parts[i] is not None:
                parts[i].wait()
                parts[i] = None


MESSAGES = [f32(MESSAGE, WIDE)] * SINGLE + [f32(2 * MESSAGE, WIDE)]
N_OUT = len(MESSAGES)
SLOT_ARRAY = pltpu.HBM((SLOTS, BLOCK, UNIT), jnp.float32)
SLOT_SPEC = HBM
ARRAY = pltpu.VMEM((ROWS, COLS), jnp.float32)
FOLDS = pltpu.VMEM((UNITS, FOLD, UNIT), jnp.float32)
HELD = pltpu.VMEM((UNITS, ROWS, UNIT), jnp.float32)


def dma(n):
    return pltpu.SemaphoreType.DMA((n,))


def unit_pack_kernel(send, whole, half, out, whole_here, half_here, folds, loads, stores):
    loads, stores = Loads(loads), Copies(stores)
    loads.start((whole, whole_here), (half, half_here))
    for u in range(UNITS):
        loads.wait(0, u)
        stores.start(whole_here.at[:, columns_of(u)], out.at[send[0, u], pl.ds(0, ROWS)])
        loads.wait(1, u)
        folds[u] = folded(half_here[:, columns_of(u)], True)
        stores.start(folds.at[u], out.at[send[0, u], pl.ds(ROWS, FOLD)])
    stores.wait()


def unit_pack(whole, half, send):
    return call(
        unit_pack_kernel,
        "unit_pack",
        [SMEM, HBM, HBM],
        SLOT_SPEC,
        SLOT_ARRAY,
        [ARRAY, ARRAY, FOLDS, dma(2 * PARTS), dma(2 * UNITS)],
        9,
        send,
        whole,
        half,
    )


def row_pack_kernel(pack, pack_rest, whole, half, *rest):
    outs, (whole_here, half_here, loads) = rest[:N_OUT], rest[N_OUT:]
    loads = Loads(loads)
    loads.start((whole, whole_here), (half, half_here))

    def unit(k, u):
        u = min(u, UNITS - 1)
        loads.wait(k, u)
        return (whole_here, half_here)[k][:, columns_of(u)]

    def tile(n):
        if n < UNITS:
            return unit(0, n)
        u = 2 * (n - UNITS)
        return jnp.where(left_lanes(ROWS), unit(1, u), swapped(unit(1, u + 1)))

    pack_rows(tile, pack, pack_rest, outs)


def row_pack(whole, half, pack):
    return call(
        row_pack_kernel,
        "row_pack",
        [VMEM, VMEM, HBM, HBM],
        [VMEM] * N_OUT,
        MESSAGES,
        [ARRAY, ARRAY, dma(2 * PARTS)],
        9,
        *pack,
        whole,
        half,
    )


def unit_row_pack_kernel(take, pack, pack_rest, recv, *rest):
    outs, (here, sems) = rest[:N_OUT], rest[N_OUT:]
    copies, arriving = Copies(sems), {}
    for i in range(0, TILES // 2, CHUNK):
        for n in [*range(i, i + CHUNK), *range(TILES // 2 + i, TILES // 2 + i + CHUNK)]:
            if n < UNITS:
                arriving[n] = copies.start(recv.at[take[0, n]], here.at[n])

    def unit(u):
        if u in arriving:
            arriving.pop(u).wait()
        return here.at[u]

    def tile(n):
        if n < UNITS:
            return unit(n)[:ROWS]
        u = 2 * (n - UNITS)
        a = unfolded(unit(u)[ROWS:], False)
        b = unfolded(unit(min(u + 1, UNITS - 1))[ROWS:], True)
        return jnp.where(left_lanes(ROWS), a, b)

    pack_rows(tile, pack, pack_rest, outs)


def unit_row_pack(recv, take, pack):
    return call(
        unit_row_pack_kernel,
        "unit_row_pack",
        [SMEM, VMEM, VMEM, ANY],
        [VMEM] * N_OUT,
        MESSAGES,
        [pltpu.VMEM((UNITS, BLOCK, UNIT), jnp.float32), dma(UNITS)],
        10,
        take,
        *pack,
        recv,
    )


def row_unit_pack_kernel(send, take, take_rest, *rest):
    parts, (out, held, folds, sems) = rest[:DP], rest[DP:]
    copies = Copies(sems)

    def put(n, tile):
        if n < UNITS:
            held[n] = tile
            copies.start(held.at[n], out.at[send[0, n], pl.ds(0, ROWS)])
            return
        for u, upper in ((2 * (n - UNITS), False), (2 * (n - UNITS) + 1, True)):
            if u < UNITS:
                folds[u] = folded(tile, upper)
                copies.start(folds.at[u], out.at[send[0, u], pl.ds(ROWS, FOLD)])

    take_rows(parts, take, take_rest, put)
    copies.wait()


def row_unit_pack(parts, send, take):
    return call(
        row_unit_pack_kernel,
        "row_unit_pack",
        [SMEM] + [VMEM] * (2 + DP),
        SLOT_SPEC,
        SLOT_ARRAY,
        [HELD, FOLDS, dma(2 * UNITS)],
        10,
        send,
        *take,
        *parts,
    )


def first_kernel(gradient, take, take_rest, *rest):
    parts, (first, half, held, half_held, sems) = rest[:DP], rest[DP:]
    copies, done = Copies(sems), set()

    def put(n, tile):
        if n < UNITS:
            columns = columns_of(n)
            moment = beta_one * tile + (1.0 - beta_one) * gradient[:, columns]
            held[:, columns] = moment
            done.add(n)
            span = n // SPAN
            if all(u in done for u in range(span * SPAN, (span + 1) * SPAN)):
                copies.start(held.at[:, span_of(span)], first.at[:, span_of(span)])
        else:
            half_held[n - UNITS] = tile
            copies.start(half_held.at[n - UNITS], half.at[n - UNITS])

    take_rows(parts, take, take_rest, put)
    copies.wait()


def first_moment(parts, take, gradient):
    return call(
        first_kernel,
        "first_moment",
        [VMEM] * (3 + DP),
        [HBM, HBM],
        [pltpu.HBM((ROWS, COLS), jnp.float32), pltpu.HBM((PAIRS, ROWS, UNIT), jnp.float32)],
        [ARRAY, pltpu.VMEM((PAIRS, ROWS, UNIT), jnp.float32), dma(TILES)],
        11,
        gradient,
        *take,
        *parts,
    )


def update_kernel(take, fixes, recv, first, half, gradient, *rest):
    outs, helds, rest = rest[:3], rest[3:6], rest[6:]
    here, first_here, half_here, gradient_here, whole_loads, unit_loads, stores = rest
    loads, whole, stores = Copies(unit_loads), Loads(whole_loads), Copies(stores)
    arrivals = [loads.start(recv.at[take[0, u]], here.at[u]) for u in range(UNITS // 3)]
    whole.start((gradient, gradient_here), (first, first_here))
    halves = loads.start(half, half_here)
    arrivals += [loads.start(recv.at[take[0, u]], here.at[u]) for u in range(UNITS // 3, UNITS)]
    for u in range(UNITS):
        arrivals[u].wait()
        columns = columns_of(u)
        weight = here[u, :ROWS]
        lower = unfolded(here[u, ROWS:], False)
        if u == 0:
            halves.wait()
        upper = half_here[u // 2]
        if u % 2 == 0:
            upper = swapped(upper)
        second = jnp.where(left_lanes(ROWS), lower, upper)
        whole.wait(0, u)
        g = gradient_here[:, columns]
        second = beta_two * second + (1.0 - beta_two) * g * g
        root = jnp.sqrt(second * fixes[1]) + epsilon
        whole.wait(1, u)
        update = first_here[:, columns] * fixes[0] / root + decay_rate * weight
        for held, out, value in zip(helds, outs, (weight - learn_rate * update, second, update)):
            held[:, columns] = value
            if u % 3 == 2:
                span = slice((u - 2) * UNIT, (u + 1) * UNIT)
                stores.start(held.at[:, span], out.at[:, span])
    stores.wait()


def weight_update(recv, take, fixes, first, half, gradient):
    return call(
        update_kernel,
        "weight_update",
        [SMEM, SMEM, ANY] + [HBM] * 3,
        [HBM] * 3,
        [f32(ROWS, COLS)] * 3,
        [ARRAY] * 3
        + [
            pltpu.VMEM((UNITS, BLOCK, UNIT), jnp.float32),
            ARRAY,
            pltpu.VMEM((PAIRS, ROWS, UNIT), jnp.float32),
            ARRAY,
            dma(2 * PARTS),
            dma(UNITS + 1),
            dma(UNITS),
        ],
        16,
        take,
        fixes,
        recv,
        first,
        half,
        gradient,
    )


def move(part, dz, dc):
    pairs = [(z * 2 + c, (z + dz) % 4 * 2 + (c + dc) % 2) for z in range(4) for c in range(2)]
    return lax.ppermute(part, "dp", pairs)


def swap_rows(parts):
    arrived = [move(part, *step) if any(step) else part for part, step in zip(parts, MOVES)]
    return arrived + [move(arrived[SINGLE][MESSAGE:], 0, 1)]


def swap_units(packed):
    packed = packed.reshape(MP, PAIR, BLOCK, UNIT)
    arrived = lax.all_to_all(
        packed, "mp", split_axis=0, concat_axis=0, tiled=True, axis_index_groups=[GRID_ORDER]
    )
    return arrived.reshape(SLOTS, BLOCK, UNIT)


def body(old_weight, old_first, old_second, gradient, old_rows, new_rows, new_units, step):
    send, take_units = unit_plan(new_units)
    pack, take = row_plan(old_rows, new_rows)
    in_hbm = functools.partial(pltpu.with_memory_space_constraint, memory_space=pltpu.HBM)
    count = step[0].astype(jnp.float32)
    fixes = jnp.stack(
        [
            1.0 / (1.0 - jnp.power(jnp.float32(beta_one), count)),
            1.0 / (1.0 - jnp.power(jnp.float32(beta_two), count)),
        ]
    )

    units = swap_units(unit_pack(in_hbm(old_first), in_hbm(old_second), send))
    rows = swap_rows(row_pack(in_hbm(old_weight), in_hbm(old_second), pack))
    packed = row_unit_pack(rows, send, take)
    units, packed = lax.optimization_barrier((units, packed))

    units_two = swap_units(packed)
    rows_two = swap_rows(unit_row_pack(units, take_units, pack))

    new_first, half = first_moment(rows_two, take, gradient)
    new_weight, new_second, update = weight_update(
        units_two, take_units, fixes, in_hbm(new_first), in_hbm(half), in_hbm(gradient)
    )
    return new_weight, new_first, new_second, update


def solution(mesh):
    return jax.shard_map(
        body,
        mesh=mesh,
        in_specs=(P("dp", "mp"), P("dp", "mp"), P("dp", "mp"), P("dp", "mp"), P(), P(), P(), P()),
        out_specs=(P("dp", "mp"), P("dp", "mp"), P("dp", "mp"), P("dp", "mp")),
        check_vma=False,
    )
```

```python
import functools

import jax
import jax.numpy as jnp
from jax import lax
from jax.experimental import pallas as pl
from jax.experimental.pallas import tpu as pltpu
from jax.sharding import PartitionSpec as P

UNIT = 128
HALF = UNIT // 2
ROWS = 192
FOLD = ROWS // 2
UNITS = 21
COLS = UNIT * UNITS
DP = 8
MP = 16
ROOM = 36
PAIR = 2
SLOTS = MP * PAIR
BLOCK = ROWS + FOLD
TILES = 32
WIDE = TILES // 2 * UNIT
MAIN = 32
REST = ROOM - MAIN
MESSAGE = 2 * ROOM
PAIRS = TILES - UNITS
CHUNK = 4
VMEM_LIMIT = 24 * 1024 * 1024

beta_one = 0.9
beta_two = 0.999
epsilon = 1e-08
learn_rate = 0.001
decay_rate = 0.1

MOVES = [(0, 0), (1, 0), (3, 0), (1, 1), (3, 1), (0, 1), (2, 0), (2, 1)]
SINGLE = 6
HBM = pl.BlockSpec(memory_space=pltpu.HBM)
ANY = pl.BlockSpec(memory_space=pl.ANY)
VMEM = pl.BlockSpec(memory_space=pltpu.VMEM)
SMEM = pl.BlockSpec(memory_space=pltpu.SMEM)


def f32(*shape):
    return jax.ShapeDtypeStruct(shape, jnp.float32)


def call(kernel, name, ins, outs, out_shape, scratch, mebibytes, *args):
    return pl.pallas_call(
        kernel,
        out_shape=out_shape,
        in_specs=ins,
        out_specs=outs,
        scratch_shapes=scratch,
        compiler_params=pltpu.CompilerParams(vmem_limit_bytes=VMEM_LIMIT),
        cost_estimate=pl.CostEstimate(
            flops=0, bytes_accessed=mebibytes * 2**20, transcendentals=0
        ),
        name=name,
    )(*args)


GRID_ORDER = [(x - a) % 4 * 4 + x for a in range(4) for x in range(4)]


def turned(row):
    n = row.shape[1]
    here = lax.broadcasted_iota(jnp.int32, (n, n), 0)
    there = lax.broadcasted_iota(jnp.int32, (n, n), 1)
    return jnp.sum(jnp.where(here == there, row, 0), axis=1, keepdims=True)


def row_plan_kernel(place, old, new, pack, pack_rest, take, take_rest):
    d = place[0]
    z, c = d // 2, d % 2
    old_mine = old[pl.ds(d, 1), :]
    new_mine = turned(new[pl.ds(d, 1), :])
    here = lax.broadcasted_iota(jnp.int32, (ROWS, ROWS), 0)
    there = lax.broadcasted_iota(jnp.int32, (ROWS, ROWS), 1)
    earlier = (here < there).astype(jnp.float32).astype(jnp.bfloat16)

    goes, comes = [], []
    for s in range(DP):
        hit = (turned(new[s : s + 1, :]) == old_mine).astype(jnp.float32)
        goes.append(jnp.max(hit, axis=0, keepdims=True))
        hit = (new_mine == old[s : s + 1, :]).astype(jnp.float32)
        comes.append(jnp.max(hit, axis=0, keepdims=True))
    both = jnp.concatenate(goes + comes, axis=0)
    before = jnp.dot(both.astype(jnp.bfloat16), earlier, preferred_element_type=jnp.float32)
    both = both.astype(jnp.int32)
    before = before.astype(jnp.int32)

    def message(dz, dc):
        at = 0
        for k, move in enumerate(MOVES):
            at = jnp.where((dz == move[0]) & (dc == move[1]), k, at)
        return at

    goes = jnp.zeros((1, ROWS), jnp.int32)
    comes = jnp.zeros((ROWS, ROWS), jnp.int32)
    for s in range(DP):
        core = (s % 2 + c) % 2
        to = message((s // 2 - z + 4) % 4, core) * 64
        goes = goes + both[s : s + 1] * (to + before[s : s + 1])
        source = message((z - s // 2 + 4) % 4, core) * 64
        value = source + before[DP + s : DP + s + 1]
        comes = comes + jnp.where(new_mine == old[s : s + 1, :], value, 0)
    comes = jnp.sum(comes, axis=1, keepdims=True)

    def places(code):
        k, rank = code >> 6, code & 63
        main = jnp.where(rank < MAIN, k * MAIN + rank, -1)
        return main, jnp.where(rank < MAIN, -1, k * 2 * REST + rank - MAIN)

    def onehot(equal):
        return equal.astype(jnp.float32).astype(jnp.bfloat16)

    def index(shape, axis):
        return lax.broadcasted_iota(jnp.int32, shape, axis)

    main, rest = places(goes)
    pack[...] = onehot(index((DP * MAIN, ROWS), 0) == main)
    rest = jnp.concatenate([rest, jnp.where(rest < 0, rest, rest + REST)], axis=1)
    pack_rest[...] = onehot(index((DP * 2 * REST, 2 * ROWS), 0) == rest)
    main, rest = places(comes)
    take[...] = onehot(index((ROWS, DP * MAIN), 1) == main)
    rest = jnp.concatenate([rest, jnp.where(rest < 0, rest, rest + REST)], axis=0)
    take_rest[...] = onehot(index((2 * ROWS, DP * 2 * REST), 1) == rest)


def row_plan(old_rows, new_rows):
    place = lax.axis_index("dp").astype(jnp.int32).reshape(1)
    shapes = [
        (DP * MAIN, ROWS),
        (DP * 2 * REST, 2 * ROWS),
        (ROWS, DP * MAIN),
        (2 * ROWS, DP * 2 * REST),
    ]
    plan = call(
        row_plan_kernel,
        "row_plan",
        [SMEM, VMEM, VMEM],
        [VMEM] * 4,
        [jax.ShapeDtypeStruct(shape, jnp.bfloat16) for shape in shapes],
        [],
        1,
        place,
        old_rows,
        new_rows,
    )
    return plan[:2], plan[2:]


def chunk_of(shard):
    return (shard - (shard >> 2) & 3) * 4 + (shard & 3)


def unit_plan_kernel(place, units, send, take):
    m = place[0]
    lane = lax.broadcasted_iota(jnp.int32, (1, UNIT), 1)
    line = lax.broadcasted_iota(jnp.int32, (UNITS, 1), 0)
    earlier = line < lane

    to_row = jnp.zeros((UNITS, UNIT), jnp.int32)
    to_column = jnp.zeros((UNITS, UNITS), jnp.int32)
    for t in range(1, MP):
        to_row = to_row + jnp.where(turned(units[t : t + 1, :]) == m * UNITS + lane, t, 0)
        to_column = to_column + jnp.where(units[t : t + 1, :] == m * UNITS + line, t, 0)
    to_row = jnp.sum(to_row, axis=0, keepdims=True)
    to_column = jnp.sum(to_column, axis=1, keepdims=True)
    rank = jnp.sum(((to_row == to_column) & earlier).astype(jnp.int32), axis=0, keepdims=True)
    send[...] = chunk_of(to_row) * PAIR + rank

    row = units[pl.ds(m, 1), :]
    column = turned(row)
    from_row, from_column = jnp.zeros_like(row), jnp.zeros_like(column)
    for t in range(1, MP):
        from_row = from_row + (row >= t * UNITS).astype(jnp.int32)
        from_column = from_column + (column >= t * UNITS).astype(jnp.int32)
    lower = (from_row == from_column) & (column < row)
    take[...] = chunk_of(from_row) * PAIR + jnp.sum(lower.astype(jnp.int32), axis=0, keepdims=True)


def unit_plan(new_units):
    place = lax.axis_index("mp").astype(jnp.int32).reshape(1)
    return call(
        unit_plan_kernel,
        "unit_plan",
        [SMEM, VMEM],
        [VMEM] * 2,
        [jax.ShapeDtypeStruct((1, n), jnp.int32) for n in (UNIT, UNITS)],
        [],
        1,
        place,
        new_units,
    )


TERMS = 2


def terms(values):
    split = []
    for _ in range(TERMS):
        split.append(values.astype(jnp.bfloat16))
        values = values - split[-1].astype(jnp.float32)
    return split


def select_rows(onehot, split):
    dot = functools.partial(jnp.dot, preferred_element_type=jnp.float32)
    return functools.reduce(lambda a, b: a + b, [dot(onehot, term) for term in split])


def columns_of(u):
    return slice(u * UNIT, (u + 1) * UNIT)


def swapped(x):
    return pltpu.roll(x, HALF, 1)


def left_lanes(rows):
    return lax.broadcasted_iota(jnp.int32, (rows, UNIT), 1) < HALF


def folded(x, upper):
    first, last = x[:FOLD], x[FOLD:]
    if upper:
        return jnp.where(left_lanes(FOLD), swapped(first), last)
    return jnp.where(left_lanes(FOLD), first, swapped(last))


def unfolded(y, upper):
    if upper:
        return jnp.concatenate([swapped(y), y], axis=0)
    return jnp.concatenate([y, swapped(y)], axis=0)


def joined(values, axis):
    return jnp.concatenate(values, axis=axis)


def pack_rows(tile, pack, pack_rest, outs):
    double = outs[SINGLE]
    outs = [*outs[:SINGLE], double.at[pl.ds(0, MESSAGE)], double.at[pl.ds(MESSAGE, MESSAGE)]]
    width = CHUNK * UNIT
    for i in range(0, TILES // 2, CHUNK):
        left = terms(joined([tile(n) for n in range(i, i + CHUNK)], 1))
        right = terms(joined([tile(TILES // 2 + n) for n in range(i, i + CHUNK)], 1))
        main = select_rows(pack[...], [joined(both, 1) for both in zip(left, right)])
        rest = select_rows(pack_rest[...], [joined(both, 0) for both in zip(left, right)])
        columns = slice(i * UNIT, (i + CHUNK) * UNIT)
        for k, out in enumerate(outs):
            rows = slice(k * MAIN, (k + 1) * MAIN)
            out[:MAIN, columns] = main[rows, :width]
            out[MAIN : 2 * MAIN, columns] = main[rows, width:]
            out[2 * MAIN :, columns] = rest[k * 2 * REST : (k + 1) * 2 * REST]


def take_rows(parts, take, take_rest, put):
    parts = [*parts[:SINGLE], parts[SINGLE].at[pl.ds(0, MESSAGE)], parts[SINGLE + 1]]
    width = CHUNK * UNIT
    for i in range(0, TILES // 2, CHUNK):
        columns = slice(i * UNIT, (i + CHUNK) * UNIT)
        left = joined([p[:MAIN, columns] for p in parts], 0)
        right = joined([p[MAIN : 2 * MAIN, columns] for p in parts], 0)
        rest = joined([p[2 * MAIN :, columns] for p in parts], 0)
        main = select_rows(take[...], terms(joined([left, right], 1)))
        rest = select_rows(take_rest[...], terms(rest))
        left, right = main[:, :width] + rest[:ROWS], main[:, width:] + rest[ROWS:]
        for k in range(CHUNK):
            put(i + k, left[:, columns_of(k)])
            put(TILES // 2 + i + k, right[:, columns_of(k)])


class Copies:
    def __init__(self, sems):
        self.sems, self.waiting = sems, []

    def start(self, source, target):
        copy = pltpu.make_async_copy(source, target, self.sems.at[len(self.waiting)])
        copy.start()
        self.waiting.append(copy)
        return copy

    def wait(self):
        for copy in self.waiting:
            copy.wait()


PARTS = 3
SPAN = UNITS // PARTS


def span_of(i):
    return slice(i * SPAN * UNIT, (i + 1) * SPAN * UNIT)


class Loads:
    def __init__(self, sems):
        self.sems, self.arrays = sems, []

    def start(self, *pairs):
        parts = [[] for _ in pairs]
        for i in range(PARTS):
            for k, (source, target) in enumerate(pairs):
                sem = self.sems.at[(len(self.arrays) + k) * PARTS + i]
                copy = pltpu.make_async_copy(
                    source.at[:, span_of(i)], target.at[:, span_of(i)], sem
                )
                copy.start()
                parts[k].append(copy)
        self.arrays += parts

    def wait(self, array, unit):
        parts = self.arrays[array]
        for i in range(unit // SPAN + 1):
            if parts[i] is not None:
                parts[i].wait()
                parts[i] = None


MESSAGES = [f32(MESSAGE, WIDE)] * SINGLE + [f32(2 * MESSAGE, WIDE)]
N_OUT = len(MESSAGES)
SLOT_ARRAY = pltpu.HBM((SLOTS, BLOCK, UNIT), jnp.float32)
SLOT_SPEC = HBM
ARRAY = pltpu.VMEM((ROWS, COLS), jnp.float32)
FOLDS = pltpu.VMEM((UNITS, FOLD, UNIT), jnp.float32)
HELD = pltpu.VMEM((UNITS, ROWS, UNIT), jnp.float32)


def dma(n):
    return pltpu.SemaphoreType.DMA((n,))


def unit_pack_kernel(send, whole, half, out, whole_here, half_here, folds, loads, stores):
    loads, stores = Loads(loads), Copies(stores)
    loads.start((whole, whole_here), (half, half_here))
    for u in range(UNITS):
        loads.wait(0, u)
        stores.start(whole_here.at[:, columns_of(u)], out.at[send[0, u], pl.ds(0, ROWS)])
        loads.wait(1, u)
        folds[u] = folded(half_here[:, columns_of(u)], True)
        stores.start(folds.at[u], out.at[send[0, u], pl.ds(ROWS, FOLD)])
    stores.wait()


def unit_pack(whole, half, send):
    return call(
        unit_pack_kernel,
        "unit_pack",
        [SMEM, HBM, HBM],
        SLOT_SPEC,
        SLOT_ARRAY,
        [ARRAY, ARRAY, FOLDS, dma(2 * PARTS), dma(2 * UNITS)],
        9,
        send,
        whole,
        half,
    )


def row_pack_kernel(pack, pack_rest, whole, half, *rest):
    outs, (whole_here, half_here, loads) = rest[:N_OUT], rest[N_OUT:]
    loads = Loads(loads)
    loads.start((whole, whole_here), (half, half_here))

    def unit(k, u):
        u = min(u, UNITS - 1)
        loads.wait(k, u)
        return (whole_here, half_here)[k][:, columns_of(u)]

    def tile(n):
        if n < UNITS:
            return unit(0, n)
        u = 2 * (n - UNITS)
        return jnp.where(left_lanes(ROWS), unit(1, u), swapped(unit(1, u + 1)))

    pack_rows(tile, pack, pack_rest, outs)


def row_pack(whole, half, pack):
    return call(
        row_pack_kernel,
        "row_pack",
        [VMEM, VMEM, HBM, HBM],
        [VMEM] * N_OUT,
        MESSAGES,
        [ARRAY, ARRAY, dma(2 * PARTS)],
        9,
        *pack,
        whole,
        half,
    )


def unit_row_pack_kernel(take, pack, pack_rest, recv, *rest):
    outs, (here, sems) = rest[:N_OUT], rest[N_OUT:]
    copies, arriving = Copies(sems), {}
    for i in range(0, TILES // 2, CHUNK):
        for n in [*range(i, i + CHUNK), *range(TILES // 2 + i, TILES // 2 + i + CHUNK)]:
            if n < UNITS:
                arriving[n] = copies.start(recv.at[take[0, n]], here.at[n])

    def unit(u):
        if u in arriving:
            arriving.pop(u).wait()
        return here.at[u]

    def tile(n):
        if n < UNITS:
            return unit(n)[:ROWS]
        u = 2 * (n - UNITS)
        a = unfolded(unit(u)[ROWS:], False)
        b = unfolded(unit(min(u + 1, UNITS - 1))[ROWS:], True)
        return jnp.where(left_lanes(ROWS), a, b)

    pack_rows(tile, pack, pack_rest, outs)


def unit_row_pack(recv, take, pack):
    return call(
        unit_row_pack_kernel,
        "unit_row_pack",
        [SMEM, VMEM, VMEM, ANY],
        [VMEM] * N_OUT,
        MESSAGES,
        [pltpu.VMEM((UNITS, BLOCK, UNIT), jnp.float32), dma(UNITS)],
        10,
        take,
        *pack,
        recv,
    )


def row_unit_pack_kernel(send, take, take_rest, *rest):
    parts, (out, held, folds, sems) = rest[:DP], rest[DP:]
    copies = Copies(sems)

    def put(n, tile):
        if n < UNITS:
            held[n] = tile
            copies.start(held.at[n], out.at[send[0, n], pl.ds(0, ROWS)])
            return
        for u, upper in ((2 * (n - UNITS), False), (2 * (n - UNITS) + 1, True)):
            if u < UNITS:
                folds[u] = folded(tile, upper)
                copies.start(folds.at[u], out.at[send[0, u], pl.ds(ROWS, FOLD)])

    take_rows(parts, take, take_rest, put)
    copies.wait()


def row_unit_pack(parts, send, take):
    return call(
        row_unit_pack_kernel,
        "row_unit_pack",
        [SMEM] + [VMEM] * (2 + DP),
        SLOT_SPEC,
        SLOT_ARRAY,
        [HELD, FOLDS, dma(2 * UNITS)],
        10,
        send,
        *take,
        *parts,
    )


def first_kernel(gradient, take, take_rest, *rest):
    parts, (first, half, held, half_held, sems) = rest[:DP], rest[DP:]
    copies, done = Copies(sems), set()

    def put(n, tile):
        if n < UNITS:
            columns = columns_of(n)
            moment = beta_one * tile + (1.0 - beta_one) * gradient[:, columns]
            held[:, columns] = moment
            done.add(n)
            span = n // SPAN
            if all(u in done for u in range(span * SPAN, (span + 1) * SPAN)):
                copies.start(held.at[:, span_of(span)], first.at[:, span_of(span)])
        else:
            half_held[n - UNITS] = tile
            copies.start(half_held.at[n - UNITS], half.at[n - UNITS])

    take_rows(parts, take, take_rest, put)
    copies.wait()


def first_moment(parts, take, gradient):
    return call(
        first_kernel,
        "first_moment",
        [VMEM] * (3 + DP),
        [HBM, HBM],
        [pltpu.HBM((ROWS, COLS), jnp.float32), pltpu.HBM((PAIRS, ROWS, UNIT), jnp.float32)],
        [ARRAY, pltpu.VMEM((PAIRS, ROWS, UNIT), jnp.float32), dma(TILES)],
        11,
        gradient,
        *take,
        *parts,
    )


def update_kernel(take, fixes, recv, first, half, gradient, *rest):
    outs, helds, rest = rest[:3], rest[3:6], rest[6:]
    here, first_here, half_here, gradient_here, whole_loads, unit_loads, stores = rest
    loads, whole, stores = Copies(unit_loads), Loads(whole_loads), Copies(stores)
    arrivals = [loads.start(recv.at[take[0, u]], here.at[u]) for u in range(UNITS // 3)]
    whole.start((gradient, gradient_here), (first, first_here))
    halves = loads.start(half, half_here)
    arrivals += [loads.start(recv.at[take[0, u]], here.at[u]) for u in range(UNITS // 3, UNITS)]
    for u in range(UNITS):
        arrivals[u].wait()
        columns = columns_of(u)
        weight = here[u, :ROWS]
        lower = unfolded(here[u, ROWS:], False)
        if u == 0:
            halves.wait()
        upper = half_here[u // 2]
        if u % 2 == 0:
            upper = swapped(upper)
        second = jnp.where(left_lanes(ROWS), lower, upper)
        whole.wait(0, u)
        g = gradient_here[:, columns]
        second = beta_two * second + (1.0 - beta_two) * g * g
        root = jnp.sqrt(second * fixes[1]) + epsilon
        whole.wait(1, u)
        update = first_here[:, columns] * fixes[0] / root + decay_rate * weight
        for held, out, value in zip(helds, outs, (weight - learn_rate * update, second, update)):
            held[:, columns] = value
            if u % 3 == 2:
                span = slice((u - 2) * UNIT, (u + 1) * UNIT)
                stores.start(held.at[:, span], out.at[:, span])
    stores.wait()


def weight_update(recv, take, fixes, first, half, gradient):
    return call(
        update_kernel,
        "weight_update",
        [SMEM, SMEM, ANY] + [HBM] * 3,
        [HBM] * 3,
        [f32(ROWS, COLS)] * 3,
        [ARRAY] * 3
        + [
            pltpu.VMEM((UNITS, BLOCK, UNIT), jnp.float32),
            ARRAY,
            pltpu.VMEM((PAIRS, ROWS, UNIT), jnp.float32),
            ARRAY,
            dma(2 * PARTS),
            dma(UNITS + 1),
            dma(UNITS),
        ],
        16,
        take,
        fixes,
        recv,
        first,
        half,
        gradient,
    )


def move(part, dz, dc):
    pairs = [(z * 2 + c, (z + dz) % 4 * 2 + (c + dc) % 2) for z in range(4) for c in range(2)]
    return lax.ppermute(part, "dp", pairs)


def swap_rows(parts):
    arrived = [move(part, *step) if any(step) else part for part, step in zip(parts, MOVES)]
    return arrived + [move(arrived[SINGLE][MESSAGE:], 0, 1)]


def swap_units(packed):
    packed = packed.reshape(MP, PAIR, BLOCK, UNIT)
    arrived = lax.all_to_all(
        packed, "mp", split_axis=0, concat_axis=0, tiled=True, axis_index_groups=[GRID_ORDER]
    )
    return arrived.reshape(SLOTS, BLOCK, UNIT)


def body(old_weight, old_first, old_second, gradient, old_rows, new_rows, new_units, step):
    send, take_units = unit_plan(new_units)
    pack, take = row_plan(old_rows, new_rows)
    in_hbm = functools.partial(pltpu.with_memory_space_constraint, memory_space=pltpu.HBM)
    count = step[0].astype(jnp.float32)
    fixes = jnp.stack(
        [
            1.0 / (1.0 - jnp.power(jnp.float32(beta_one), count)),
            1.0 / (1.0 - jnp.power(jnp.float32(beta_two), count)),
        ]
    )

    units = swap_units(unit_pack(in_hbm(old_first), in_hbm(old_second), send))
    rows = swap_rows(row_pack(in_hbm(old_weight), in_hbm(old_second), pack))
    packed = row_unit_pack(rows, send, take)
    units, packed = lax.optimization_barrier((units, packed))

    units_two = swap_units(packed)
    rows_two = swap_rows(unit_row_pack(units, take_units, pack))

    new_first, half = first_moment(rows_two, take, gradient)
    new_weight, new_second, update = weight_update(
        units_two, take_units, fixes, in_hbm(new_first), in_hbm(half), in_hbm(gradient)
    )
    return new_weight, new_first, new_second, update


def solution(mesh):
    return jax.shard_map(
        body,
        mesh=mesh,
        in_specs=(P("dp", "mp"), P("dp", "mp"), P("dp", "mp"), P("dp", "mp"), P(), P(), P(), P()),
        out_specs=(P("dp", "mp"), P("dp", "mp"), P("dp", "mp"), P("dp", "mp")),
        check_vma=False,
    )
```
